32 devices in a mesh: rows: 2 (over x), res: 16 (over z, y, core).
Axes of the slice: x: 2, y: 2, z: 4, core: 2. Of those that a mesh axis runs over, the one named last changes fastest.
Arguments:
- source_alignment_rows: bfloat16 [128, 256, 256], P('rows', 'res'), may hold values from -120 to 120
- pairs: int32 [6, 128], P(None, 'rows'), may hold values from -1 to 127, as said below
- chain_first_residue: int32 [6], replicated, may hold values from 0 to 235, as said below
- gap_embedding: bfloat16 [256], replicated, may hold values from -4 to 4
- layer_norm_gain: bfloat16 [256], replicated, may hold values from 0.099609375 to 1.8984375
- layer_norm_bias: bfloat16 [256], replicated, may hold values from -3 to 3
- projection_weight: bfloat16 [256, 8, 128], replicated, may hold values from -0.375 to 0.375
- gate_bias_heads: bfloat16 [256], replicated, may hold values from -4 to 4
- pair_bias_logits: bfloat16 [8, 256, 256], P(None, 'res'), may hold values from -6 to 320
- output_weight: bfloat16 [256, 256], replicated, may hold values from -0.375 to 0.375
- output_bias: bfloat16 [256], replicated, may hold values from -3 to 3
Outputs:
- update: bfloat16 [128, 256, 256], P('rows', 'res')
The draws below stay inside these ranges and needn't reach their ends.
Inputs may be any that keep to these rules, and one draw needn't show every extreme that they name: `pairs`: within one chain each source row is named at most once; chain 0 has no gaps. For each chain and each aligned block of 64 joint rows, at most 32 entries name rows of one aligned block of 64 source rows, and exactly 32 in some block. chain_first_residue[0] is 0, the starts rise, chain k holds residues from its start up to the next start (the last up to 256), and each chain has at least 21 residues; the last chain has exactly that many.
All inputs are finite; a program needn't handle non-finite values.
Results may differ from the reference program's by a relative error of at most 0.012.
Values may be sent and summed in bfloat16 or wider, within the bound.
No kernel may reach another device: no remote copies, remote signals or barrier semaphores. Data moves between devices by JAX's collectives and lax.ppermute only.
A program may use at most 64 MiB of HBM per device.

```python
import math
import jax
import jax.numpy as jnp
from jax import lax

C_M = 256
HEADS = 8
HEAD_DIM = 32
CHAINS = 6
JOINT_DEV = 64
TOTAL_ROWS = 128
RESIDUES = 256
CAP = 32


def draw_source_alignment_rows(key, part):
    key = jax.random.fold_in(key, 11)
    base_key, chan_key, cell_key = jax.random.split(key, 3)
    array_shape = (TOTAL_ROWS, RESIDUES, C_M)
    chan_scale = jnp.exp(jax.random.uniform(chan_key, (C_M,), jnp.float32, 0.0, math.log(10.0)))
    cell_scale = jnp.exp(jax.random.uniform(cell_key, (TOTAL_ROWS, RESIDUES, 1), jnp.float32, 0.0, math.log(3.0)))
    base = jnp.clip(jax.random.normal(base_key, array_shape, jnp.float32), -4.0, 4.0)
    return jnp.clip(base * chan_scale * cell_scale, -120.0, 120.0).astype(jnp.bfloat16)


def draw_pairs(key, part):
    key = jax.random.fold_in(key, 23)
    owners = TOTAL_ROWS // JOINT_DEV

    def chain_list(chain_index):
        chain_key = jax.random.fold_in(key, chain_index)
        offset_key, slot_key, place_key, gap_key = jax.random.split(chain_key, 4)
        offsets = jax.random.permutation(offset_key, owners)
        dest_ids = jnp.arange(owners, dtype=jnp.int32)
        source_dev = (dest_ids[:, None] + offsets[None, :]) % owners
        slot_scores = jax.random.randint(slot_key, (owners, owners, CAP), 0, 1 << 20) * CAP + jnp.arange(CAP, dtype=jnp.int32)
        slot_order = jnp.argsort(slot_scores, axis=-1).astype(jnp.int32)
        source_local = jnp.arange(owners, dtype=jnp.int32)[None, :, None] * CAP + slot_order
        flat_rows = (source_dev[:, :, None] * JOINT_DEV + source_local).reshape(owners, JOINT_DEV)
        place_scores = jax.random.randint(place_key, (owners, JOINT_DEV), 0, 1 << 20) * JOINT_DEV + jnp.arange(JOINT_DEV, dtype=jnp.int32)
        place_order = jnp.argsort(place_scores, axis=-1)
        placed = jnp.take_along_axis(flat_rows, place_order, axis=1)
        gap_draw = jax.random.randint(gap_key, (owners, JOINT_DEV), 0, 8)
        is_gap = (gap_draw < (dest_ids % 4)[:, None]) & (chain_index > 0)
        return jnp.where(is_gap, -1, placed).reshape(TOTAL_ROWS)
    return jnp.stack([chain_list(chain_index) for chain_index in range(CHAINS)]).astype(jnp.int32)


def draw_chain_first_residue(key, part):
    key = jax.random.fold_in(key, 37)
    least = RESIDUES // (2 * CHAINS)
    spare = RESIDUES - CHAINS * least
    cuts = jnp.sort(jax.random.randint(key, (CHAINS - 1,), 0, spare + 1))
    cuts = cuts.at[CHAINS - 2].set(spare)
    later = jnp.arange(1, CHAINS, dtype=jnp.int32) * least + cuts
    return jnp.concatenate([jnp.zeros((1,), jnp.int32), later.astype(jnp.int32)])


def draw_pair_bias_logits(key, part):
    key = jax.random.fold_in(key, 41)
    base_key = jax.random.fold_in(key, 0)
    array_shape = (HEADS, RESIDUES, RESIDUES)
    values = jnp.clip(1.5 * jax.random.normal(base_key, array_shape, jnp.float32), -6.0, 6.0)
    return values.astype(jnp.bfloat16)


def noise(rng, dims, width, reach, kind=jnp.bfloat16):
    return jnp.clip(width * jax.random.normal(rng, dims, jnp.float32), -reach, reach).astype(kind)


def setup_inputs(seed: int = 0) -> dict:
    keys = jax.random.split(jax.random.key(seed), 12)
    return {
        "source_alignment_rows": draw_source_alignment_rows(jax.random.fold_in(keys[11], 71), 0),
        "pairs": draw_pairs(jax.random.fold_in(keys[11], 71), 0),
        "chain_first_residue": draw_chain_first_residue(jax.random.fold_in(keys[11], 71), 0),
        "gap_embedding": noise(keys[3], (C_M,), 1.0, 4.0),
        "layer_norm_gain": jnp.clip(1.0 + 0.18 * jax.random.normal(keys[4], (C_M,), jnp.float32), 0.099609375, 1.8984375).astype(jnp.bfloat16),
        "layer_norm_bias": noise(keys[5], (C_M,), 0.5, 3.0),
        "projection_weight": noise(keys[6], (C_M, HEADS, 4 * HEAD_DIM), C_M ** -0.5, 0.375),
        "gate_bias_heads": noise(keys[7], (C_M,), 1.0, 4.0),
        "pair_bias_logits": draw_pair_bias_logits(jax.random.fold_in(keys[11], 71), 0),
        "output_weight": noise(keys[9], (C_M, C_M), C_M ** -0.5, 0.375),
        "output_bias": noise(keys[10], (C_M,), 0.5, 3.0),
    }


norm_eps = 1e-05
ref_block = 16

def layer_norm(values, gain, shift):
    widened = values.astype(jnp.float32)
    center = lax.optimization_barrier(jnp.mean(widened, axis=-1, keepdims=True))
    spread = lax.optimization_barrier(jnp.mean(jnp.square(widened - center), axis=-1, keepdims=True))
    scaled = (widened - center) * lax.rsqrt(spread + norm_eps)
    return (scaled * gain.astype(jnp.float32) + shift.astype(jnp.float32)).astype(jnp.bfloat16)

def reference(source_alignment_rows, pairs, chain_first_residue, gap_embedding, layer_norm_gain, layer_norm_bias, projection_weight, gate_bias_heads, pair_bias_logits, output_weight, output_bias):
    column_indices = jnp.arange(RESIDUES, dtype=jnp.int32)
    chain_of = lax.optimization_barrier(jnp.sum((column_indices[:, None] >= chain_first_residue[None, 1:]).astype(jnp.int32), axis=1)).astype(jnp.int32)
    column_lists = pairs[chain_of]
    proj_weight = projection_weight.astype(jnp.float32)
    out_weight = output_weight.astype(jnp.float32).reshape(HEADS, HEAD_DIM, C_M)
    bias_wide = pair_bias_logits.astype(jnp.float32)
    gate_shift = gate_bias_heads.astype(jnp.float32).reshape(HEADS, 1, HEAD_DIM)
    query_scale = HEAD_DIM ** (-0.5)

    def one_block(first_row):
        selected_rows = lax.dynamic_slice_in_dim(column_lists, first_row, ref_block, 1).T
        gathered_rows = source_alignment_rows[jnp.maximum(selected_rows, 0), column_indices[None, :]]
        joint_rows = jnp.where((selected_rows >= 0)[..., None], gathered_rows, gap_embedding[None, None, :])
        normed = layer_norm(joint_rows, layer_norm_gain, layer_norm_bias)
        projected = jnp.einsum('rcm,mhe->rhce', normed.astype(jnp.float32), proj_weight)
        queries = (projected[..., :HEAD_DIM] * query_scale).astype(jnp.bfloat16)
        key_rows = projected[..., HEAD_DIM:2 * HEAD_DIM].astype(jnp.bfloat16)
        value_rows = projected[..., 2 * HEAD_DIM:3 * HEAD_DIM].astype(jnp.bfloat16)
        gate_rows = jax.nn.sigmoid(projected[..., 3 * HEAD_DIM:] + gate_shift[None]).astype(jnp.bfloat16)
        scores = jnp.einsum('rhqd,rhkd->rhqk', queries.astype(jnp.float32), key_rows.astype(jnp.float32)) + bias_wide[None]
        highest = lax.optimization_barrier(jnp.max(scores, axis=-1, keepdims=True))
        lifted = jnp.exp(scores - highest)
        weights = (lifted / lax.optimization_barrier(jnp.sum(lifted, axis=-1, keepdims=True))).astype(jnp.bfloat16)
        summed = jnp.einsum('rhqk,rhkd->rhqd', weights.astype(jnp.float32), value_rows.astype(jnp.float32))
        attended = (summed * gate_rows.astype(jnp.float32)).astype(jnp.bfloat16)
        update = jnp.einsum('rhqd,hdm->rqm', attended.astype(jnp.float32), out_weight) + output_bias.astype(jnp.float32)
        return update.astype(jnp.bfloat16)
    firsts = jnp.arange(TOTAL_ROWS // ref_block, dtype=jnp.int32) * ref_block
    blocks = lax.map(one_block, firsts)
    return blocks.reshape(TOTAL_ROWS, RESIDUES, C_M)
```

```python
import functools
import math

import jax
import jax.numpy as jnp
from jax import lax
from jax.experimental import pallas as pl
from jax.experimental.pallas import tpu as pltpu
from jax.sharding import PartitionSpec as P

norm_eps = 1e-05
log2e = math.log2(math.e)
parts = 1


def pick_kernel(owners, first_row, pairs_ref, first_ref, gap_ref, *refs):
    blocks, (out_ref, held, sems) = refs[:owners], refs[-3:]
    local_rows, local_columns, channels = blocks[0].shape
    part_rows = out_ref.shape[0]
    pieces = sems.shape[0]
    piece_rows = part_rows // pieces
    chains = first_ref.shape[0]
    shift = local_rows.bit_length() - 1
    assert local_rows == 1 << shift
    me = lax.axis_index("rows")
    start = lax.axis_index("res") * local_columns
    low, high = jnp.int32(0), jnp.int32(0)
    for k in range(1, chains):
        low += (first_ref[k] <= start).astype(jnp.int32)
        high += (first_ref[k] <= start + local_columns - 1).astype(jnp.int32)
    edge = first_ref[high] - start
    in_high = lax.broadcasted_iota(jnp.int32, (local_columns, channels), 0) >= edge
    gap = gap_ref[...].astype(jnp.float32).reshape(1, channels)
    gap = jnp.broadcast_to(gap, (local_columns, channels))
    names = [lax.rem(me - k + owners, owners) for k in range(owners)]

    def cells(row):
        owner = row >> shift
        within = row & (local_rows - 1)
        found = blocks[0][within].astype(jnp.float32)
        for k in range(1, owners):
            found = jnp.where(owner == names[k], blocks[k][within].astype(jnp.float32), found)
        return jnp.where(row >= 0, found, gap)

    def one_row(s, carry):
        row = first_row + s
        picked = jnp.where(in_high, cells(pairs_ref[high, row]), cells(pairs_ref[low, row]))
        held[s] = picked.astype(jnp.bfloat16)
        return carry

    copies = []
    for k in range(pieces):
        rows = pl.ds(k * piece_rows, piece_rows)
        lax.fori_loop(k * piece_rows, (k + 1) * piece_rows, one_row, 0, unroll=piece_rows)
        copies.append(pltpu.make_async_copy(held.at[rows], out_ref.at[rows], sems.at[k]))
        copies[-1].start()
    for copy in copies:
        copy.wait()


def pick(part, parts, pairs, chain_first_residue, gap, blocks, earlier):
    owners = len(blocks)
    local_rows, local_columns, channels = blocks[0].shape
    part_rows = local_rows // parts
    pieces = part_rows // 16
    smem = pl.BlockSpec(memory_space=pltpu.SMEM)
    vmem = pl.BlockSpec(memory_space=pltpu.VMEM)
    anywhere = pl.BlockSpec(memory_space=pl.ANY)
    block_bytes = local_rows * local_columns * channels * 2
    shape = (part_rows, local_columns, channels)
    return pl.pallas_call(
        functools.partial(pick_kernel, owners, part * part_rows),
        out_shape=jax.ShapeDtypeStruct(shape, jnp.bfloat16),
        in_specs=[smem, smem, vmem] + [vmem] * owners + [anywhere] * len(earlier),
        out_specs=anywhere,
        scratch_shapes=[pltpu.VMEM(shape, jnp.bfloat16), pltpu.SemaphoreType.DMA((pieces,))],
        compiler_params=pltpu.CompilerParams(vmem_limit_bytes=(owners + 4) * block_bytes),
        name="pick_joint",
    )(pairs, chain_first_residue, gap, *blocks, *earlier)


def bias_kernel(order, near_ref, far_ref, *refs):
    rows, gate_ref, (out_ref, vectors_ref, held) = refs[:3], refs[3], refs[-3:]
    me = lax.axis_index("res")
    half, heads, block, _ = near_ref.shape
    for place, flip in enumerate(order):
        source = near_ref if place < half else far_ref
        first = pl.multiple_of((me ^ flip) * block, block)
        held[:, pl.ds(first, block), :] = source[place % half].astype(jnp.float32)

    def one_head(h, carry):
        out_ref[h] = held[h].T * log2e
        return carry

    lax.fori_loop(0, heads, one_head, 0)
    width = gate_ref.shape[0]
    for place, ref in enumerate(rows):
        vectors_ref[place : place + 1] = ref[...].astype(jnp.float32).reshape(1, width)
    gate = gate_ref[...].astype(jnp.float32).reshape(1, width)
    vectors_ref[8:] = jnp.broadcast_to(gate, (width, width)).T


def gather_bias(shard):
    members = lax.axis_size("res")

    def swap(piece, flip):
        return lax.ppermute(piece, "res", [(i, i ^ flip) for i in range(members)])

    far, next_far = members // 2, members // 4
    shard = shard[None]
    pieces = [shard]
    order = [0]
    for flip in (far, next_far, far + next_far):
        pieces.append(swap(shard, flip))
        order.append(flip)
    flip = members // 8
    while flip > 1:
        pieces += [swap(piece, flip) for piece in pieces]
        order += [place ^ flip for place in order]
        flip //= 2
    near = jnp.concatenate(pieces, axis=0)
    return near, swap(near, 1), order + [place ^ 1 for place in order]


def order_bias(near, other, order, vectors, earlier):
    half, heads, block, keys = near.shape
    width = vectors[-1].shape[0]
    vmem = pl.BlockSpec(memory_space=pltpu.VMEM)
    anywhere = pl.BlockSpec(memory_space=pl.ANY)
    return pl.pallas_call(
        functools.partial(bias_kernel, order),
        out_shape=[
            jax.ShapeDtypeStruct((heads, keys, 2 * half * block), jnp.float32),
            jax.ShapeDtypeStruct((8 + width, width), jnp.float32),
        ],
        in_specs=[vmem] * (2 + len(vectors)) + [anywhere] * len(earlier),
        out_specs=[vmem] * 2,
        scratch_shapes=[pltpu.VMEM((heads, 2 * half * block, keys), jnp.float32)],
        compiler_params=pltpu.CompilerParams(vmem_limit_bytes=14 << 20),
        name="order_bias",
    )(near, other, *vectors, *earlier)


def weights_kernel(heads, weight_ref, weights_ref):
    width = weight_ref.shape[1] // 4
    depth = width // heads
    turned = weight_ref[...].T
    kinds = []
    for kind in range(4):
        rows = [turned[(h * 4 + kind) * depth : (h * 4 + kind + 1) * depth] for h in range(heads)]
        kinds.append(jnp.concatenate(rows, axis=0))
    for place, kind in enumerate((kinds[0], kinds[2], kinds[3], kinds[1].T)):
        weights_ref[place * width : (place + 1) * width] = kind


def turn_weights(projection_weight):
    channels, heads, four = projection_weight.shape
    width = heads * four // 4
    vmem = pl.BlockSpec(memory_space=pltpu.VMEM)
    return pl.pallas_call(
        functools.partial(weights_kernel, heads),
        out_shape=jax.ShapeDtypeStruct((4 * width, channels), jnp.bfloat16),
        in_specs=[vmem],
        out_specs=vmem,
        compiler_params=pltpu.CompilerParams(vmem_limit_bytes=8 << 20),
        name="turn_weights",
    )(projection_weight.reshape(channels, heads * four))


def attend_kernel(cells_ref, weights_ref, out_weight_ref, vectors_ref, bias_ref, out_ref):
    senders, rows, block, channels = cells_ref.shape
    residues = senders * block
    heads = bias_ref.shape[0]
    width = weights_ref.shape[0] // 4
    depth = width // heads
    ones = jnp.ones((16, residues), jnp.bfloat16)

    def begin(r):
        wide = cells_ref[:, r].reshape(residues, channels).astype(jnp.float32)
        center = jnp.mean(wide, axis=-1, keepdims=True)
        wide = wide - center
        spread = jnp.mean(jnp.square(wide), axis=-1, keepdims=True)
        normed = wide * lax.rsqrt(spread + norm_eps) * vectors_ref[0:1] + vectors_ref[1:2]
        normed = normed.astype(jnp.bfloat16)
        keys = jnp.dot(
            normed, weights_ref[3 * width :], preferred_element_type=jnp.float32
        )
        rest = lax.dot_general(
            weights_ref[: 3 * width], normed, (((1,), (1,)), ((), ())),
            preferred_element_type=jnp.float32,
        )
        queries = (rest[:width] * (depth**-0.5 * log2e)).astype(jnp.bfloat16)
        values = rest[width : 2 * width].astype(jnp.bfloat16)
        gates = 0.5 + 0.5 * jnp.tanh(0.5 * (rest[2 * width :] + vectors_ref[8:]))
        return keys.astype(jnp.bfloat16), queries, values, gates

    def score(row, h):
        keys, queries = row[:2]
        low, high = h * depth, (h + 1) * depth
        scores = jnp.dot(keys[:, low:high], queries[low:high], preferred_element_type=jnp.float32)
        return scores + bias_ref[h]

    def weigh(row, h, scores):
        values, gates = row[2:]
        low, high = h * depth, (h + 1) * depth
        highest = jnp.max(scores, axis=0, keepdims=True)
        lifted = jnp.exp2(scores - highest).astype(jnp.bfloat16)
        left = jnp.concatenate([values[low:high], ones], axis=0)
        summed = jnp.dot(left, lifted, preferred_element_type=jnp.float32)
        inverse = 1.0 / summed[depth : depth + 1]
        return (summed[:depth] * (gates[low:high] * inverse)).astype(jnp.bfloat16)

    def finish(r, heads_out):
        attended = jnp.concatenate(heads_out, axis=0).T
        update = jnp.dot(attended, out_weight_ref[...], preferred_element_type=jnp.float32)
        update = (update + vectors_ref[2:3]).astype(jnp.bfloat16)
        out_ref[:, r] = update.reshape(senders, block, channels)

    steps = [(r, h) for r in range(rows) for h in range(heads)]
    begun = {0: begin(0)}
    scores = score(begun[0], 0)
    done = {r: [] for r in range(rows)}
    for (r, h), later in zip(steps, steps[1:] + [None]):
        if h == heads // 2 and r + 1 < rows:
            begun[r + 1] = begin(r + 1)
        later_scores = score(begun[later[0]], later[1]) if later else None
        if h == 0 and r:
            finish(r - 1, done[r - 1])
        done[r].append(weigh(begun[r], h, scores))
        scores = later_scores
    finish(rows - 1, done[rows - 1])


def attend(cells, weights, out_weight, vectors, bias):
    vmem = pl.BlockSpec(memory_space=pltpu.VMEM)
    return pl.pallas_call(
        attend_kernel,
        out_shape=jax.ShapeDtypeStruct(cells.shape, jnp.bfloat16),
        in_specs=[vmem] * 5,
        out_specs=vmem,
        compiler_params=pltpu.CompilerParams(vmem_limit_bytes=24 << 20),
        name="attend_rows",
    )(cells, weights, out_weight, vectors, bias)


def local(
    source_alignment_rows,
    pairs,
    chain_first_residue,
    gap_embedding,
    layer_norm_gain,
    layer_norm_bias,
    projection_weight,
    gate_bias_heads,
    pair_bias_logits,
    output_weight,
    output_bias,
):
    local_rows, local_columns, channels = source_alignment_rows.shape
    owners = lax.axis_size("rows")
    members = lax.axis_size("res")
    near, other, order = gather_bias(pair_bias_logits)
    blocks = [source_alignment_rows]
    for hop in range(1, owners):
        blocks.append(
            lax.ppermute(
                source_alignment_rows, "rows", [(i, (i + hop) % owners) for i in range(owners)]
            )
        )
    weights = turn_weights(projection_weight)
    arrived = []
    for part in range(parts):
        picked = pick(part, parts, pairs, chain_first_residue, gap_embedding, blocks, (weights,))
        arrived.append(lax.all_to_all(picked, "res", split_axis=0, concat_axis=0, tiled=True))
    bias, vectors = order_bias(
        near,
        other,
        order,
        (layer_norm_gain, layer_norm_bias, output_bias, gate_bias_heads),
        (weights, output_weight),
    )
    results = []
    for cells in arrived:
        part_rows = cells.shape[0]
        update = attend(
            cells.reshape(members, part_rows // members, local_columns, channels),
            weights,
            output_weight,
            vectors,
            bias,
        )
        update = update.reshape(part_rows, local_columns, channels)
        results.append(lax.all_to_all(update, "res", split_axis=0, concat_axis=0, tiled=True))
    return jnp.concatenate(results, axis=0)


def solution(mesh):
    return jax.shard_map(
        local,
        mesh=mesh,
        in_specs=(
            P("rows", "res", None),
            P(None, "rows"),
            P(),
            P(),
            P(),
            P(),
            P(),
            P(),
            P(None, "res", None),
            P(),
            P(),
        ),
        out_specs=P("rows", "res", None),
        check_vma=False,
    )
```

```python
import functools
import math

import jax
import jax.numpy as jnp
from jax import lax
from jax.experimental import pallas as pl
from jax.experimental.pallas import tpu as pltpu
from jax.sharding import PartitionSpec as P

norm_eps = 1e-05
log2e = math.log2(math.e)
parts = 1


def pick_kernel(owners, first_row, pairs_ref, first_ref, gap_ref, *refs):
    blocks, (out_ref, held, sems) = refs[:owners], refs[-3:]
    local_rows, local_columns, channels = blocks[0].shape
    part_rows = out_ref.shape[0]
    pieces = sems.shape[0]
    piece_rows = part_rows // pieces
    chains = first_ref.shape[0]
    shift = local_rows.bit_length() - 1
    assert local_rows == 1 << shift
    me = lax.axis_index("rows")
    start = lax.axis_index("res") * local_columns
    low, high = jnp.int32(0), jnp.int32(0)
    for k in range(1, chains):
        low += (first_ref[k] <= start).astype(jnp.int32)
        high += (first_ref[k] <= start + local_columns - 1).astype(jnp.int32)
    edge = first_ref[high] - start
    in_high = lax.broadcasted_iota(jnp.int32, (local_columns, channels), 0) >= edge
    gap = gap_ref[...].astype(jnp.float32).reshape(1, channels)
    gap = jnp.broadcast_to(gap, (local_columns, channels))
    names = [lax.rem(me - k + owners, owners) for k in range(owners)]

    def cells(row):
        owner = row >> shift
        within = row & (local_rows - 1)
        found = blocks[0][within].astype(jnp.float32)
        for k in range(1, owners):
            found = jnp.where(owner == names[k], blocks[k][within].astype(jnp.float32), found)
        return jnp.where(row >= 0, found, gap)

    def one_row(s, carry):
        row = first_row + s
        picked = jnp.where(in_high, cells(pairs_ref[high, row]), cells(pairs_ref[low, row]))
        held[s] = picked.astype(jnp.bfloat16)
        return carry

    copies = []
    for k in range(pieces):
        rows = pl.ds(k * piece_rows, piece_rows)
        lax.fori_loop(k * piece_rows, (k + 1) * piece_rows, one_row, 0, unroll=piece_rows)
        copies.append(pltpu.make_async_copy(held.at[rows], out_ref.at[rows], sems.at[k]))
        copies[-1].start()
    for copy in copies:
        copy.wait()


def pick(part, parts, pairs, chain_first_residue, gap, blocks, earlier):
    owners = len(blocks)
    local_rows, local_columns, channels = blocks[0].shape
    part_rows = local_rows // parts
    pieces = part_rows // 16
    smem = pl.BlockSpec(memory_space=pltpu.SMEM)
    vmem = pl.BlockSpec(memory_space=pltpu.VMEM)
    anywhere = pl.BlockSpec(memory_space=pl.ANY)
    block_bytes = local_rows * local_columns * channels * 2
    shape = (part_rows, local_columns, channels)
    return pl.pallas_call(
        functools.partial(pick_kernel, owners, part * part_rows),
        out_shape=jax.ShapeDtypeStruct(shape, jnp.bfloat16),
        in_specs=[smem, smem, vmem] + [vmem] * owners + [anywhere] * len(earlier),
        out_specs=anywhere,
        scratch_shapes=[pltpu.VMEM(shape, jnp.bfloat16), pltpu.SemaphoreType.DMA((pieces,))],
        compiler_params=pltpu.CompilerParams(vmem_limit_bytes=(owners + 4) * block_bytes),
        name="pick_joint",
    )(pairs, chain_first_residue, gap, *blocks, *earlier)


def bias_kernel(order, near_ref, far_ref, *refs):
    rows, gate_ref, (out_ref, vectors_ref, held) = refs[:3], refs[3], refs[-3:]
    me = lax.axis_index("res")
    half, heads, block, _ = near_ref.shape
    for place, flip in enumerate(order):
        source = near_ref if place < half else far_ref
        first = pl.multiple_of((me ^ flip) * block, block)
        held[:, pl.ds(first, block), :] = source[place % half].astype(jnp.float32)

    def one_head(h, carry):
        out_ref[h] = held[h].T * log2e
        return carry

    lax.fori_loop(0, heads, one_head, 0)
    width = gate_ref.shape[0]
    for place, ref in enumerate(rows):
        vectors_ref[place : place + 1] = ref[...].astype(jnp.float32).reshape(1, width)
    gate = gate_ref[...].astype(jnp.float32).reshape(1, width)
    vectors_ref[8:] = jnp.broadcast_to(gate, (width, width)).T


def gather_bias(shard):
    members = lax.axis_size("res")

    def swap(piece, flip):
        return lax.ppermute(piece, "res", [(i, i ^ flip) for i in range(members)])

    far, next_far = members // 2, members // 4
    shard = shard[None]
    pieces = [shard]
    order = [0]
    for flip in (far, next_far, far + next_far):
        pieces.append(swap(shard, flip))
        order.append(flip)
    flip = members // 8
    while flip > 1:
        pieces += [swap(piece, flip) for piece in pieces]
        order += [place ^ flip for place in order]
        flip //= 2
    near = jnp.concatenate(pieces, axis=0)
    return near, swap(near, 1), order + [place ^ 1 for place in order]


def order_bias(near, other, order, vectors, earlier):
    half, heads, block, keys = near.shape
    width = vectors[-1].shape[0]
    vmem = pl.BlockSpec(memory_space=pltpu.VMEM)
    anywhere = pl.BlockSpec(memory_space=pl.ANY)
    return pl.pallas_call(
        functools.partial(bias_kernel, order),
        out_shape=[
            jax.ShapeDtypeStruct((heads, keys, 2 * half * block), jnp.float32),
            jax.ShapeDtypeStruct((8 + width, width), jnp.float32),
        ],
        in_specs=[vmem] * (2 + len(vectors)) + [anywhere] * len(earlier),
        out_specs=[vmem] * 2,
        scratch_shapes=[pltpu.VMEM((heads, 2 * half * block, keys), jnp.float32)],
        compiler_params=pltpu.CompilerParams(vmem_limit_bytes=14 << 20),
        name="order_bias",
    )(near, other, *vectors, *earlier)


def weights_kernel(heads, weight_ref, weights_ref):
    width = weight_ref.shape[1] // 4
    depth = width // heads
    turned = weight_ref[...].T
    kinds = []
    for kind in range(4):
        rows = [turned[(h * 4 + kind) * depth : (h * 4 + kind + 1) * depth] for h in range(heads)]
        kinds.append(jnp.concatenate(rows, axis=0))
    for place, kind in enumerate((kinds[0], kinds[2], kinds[3], kinds[1].T)):
        weights_ref[place * width : (place + 1) * width] = kind


def turn_weights(projection_weight):
    channels, heads, four = projection_weight.shape
    width = heads * four // 4
    vmem = pl.BlockSpec(memory_space=pltpu.VMEM)
    return pl.pallas_call(
        functools.partial(weights_kernel, heads),
        out_shape=jax.ShapeDtypeStruct((4 * width, channels), jnp.bfloat16),
        in_specs=[vmem],
        out_specs=vmem,
        compiler_params=pltpu.CompilerParams(vmem_limit_bytes=8 << 20),
        name="turn_weights",
    )(projection_weight.reshape(channels, heads * four))


def attend_kernel(
    cells_ref, weights_ref, out_weight_ref, vectors_ref, bias_ref, out_ref, scores_ref
):
    senders, rows, block, channels = cells_ref.shape
    residues = senders * block
    heads = bias_ref.shape[0]
    width = weights_ref.shape[0] // 4
    depth = width // heads
    ones = jnp.ones((16, residues), jnp.bfloat16)
    group = min(128, width)
    head_of = lax.broadcasted_iota(jnp.int32, (1, group), 1) // depth
    masks = [(head_of == h).astype(jnp.bfloat16) for h in range(group // depth)]

    def begin(r):
        wide = cells_ref[:, r].reshape(residues, channels).astype(jnp.float32)
        center = jnp.mean(wide, axis=-1, keepdims=True)
        wide = wide - center
        spread = jnp.mean(jnp.square(wide), axis=-1, keepdims=True)
        normed = wide * lax.rsqrt(spread + norm_eps) * vectors_ref[0:1] + vectors_ref[1:2]
        normed = normed.astype(jnp.bfloat16)
        keys = jnp.dot(
            normed, weights_ref[3 * width :], preferred_element_type=jnp.float32
        )
        rest = lax.dot_general(
            weights_ref[: 3 * width], normed, (((1,), (1,)), ((), ())),
            preferred_element_type=jnp.float32,
        )
        queries = (rest[:width] * (depth**-0.5 * log2e)).astype(jnp.bfloat16)
        values = rest[width : 2 * width].astype(jnp.bfloat16)
        keys = keys.astype(jnp.bfloat16)
        for k in range(width // group):
            lanes = slice(k * group, (k + 1) * group)
            stack = jnp.concatenate([keys[:, lanes] * mask for mask in masks], axis=0)
            bias = bias_ref[k * len(masks) : (k + 1) * len(masks)]
            scores = jnp.dot(stack, queries[lanes], preferred_element_type=jnp.float32)
            scores_ref[r % 2, k] = scores + bias.reshape(scores.shape)
        gates = 0.5 + 0.5 * jnp.tanh(0.5 * (rest[2 * width :] + vectors_ref[8:]))
        return values, gates

    def weigh(r, h):
        values, gates = begun[r]
        low, high = h * depth, (h + 1) * depth
        first = low % group // depth * residues
        scores = scores_ref[r % 2, low // group, first : first + residues]
        highest = jnp.max(scores, axis=0, keepdims=True)
        lifted = jnp.exp2(scores - highest).astype(jnp.bfloat16)
        left = jnp.concatenate([values[low:high], ones], axis=0)
        summed = jnp.dot(left, lifted, preferred_element_type=jnp.float32)
        inverse = 1.0 / summed[depth : depth + 1]
        return (summed[:depth] * (gates[low:high] * inverse)).astype(jnp.bfloat16)

    def finish(r, heads_out):
        attended = jnp.concatenate(heads_out, axis=0).T
        update = jnp.dot(attended, out_weight_ref[...], preferred_element_type=jnp.float32)
        update = (update + vectors_ref[2:3]).astype(jnp.bfloat16)
        out_ref[:, r] = update.reshape(senders, block, channels)

    begun = {0: begin(0)}
    done = {r: [] for r in range(rows)}
    for r in range(rows):
        for h in range(heads):
            if h == heads // 2 and r + 1 < rows:
                begun[r + 1] = begin(r + 1)
            done[r].append(weigh(r, h))
            if h == 0 and r:
                finish(r - 1, done[r - 1])
    finish(rows - 1, done[rows - 1])


def attend(cells, weights, out_weight, vectors, bias):
    heads, residues, _ = bias.shape
    width = weights.shape[0] // 4
    group = min(128, width)
    vmem = pl.BlockSpec(memory_space=pltpu.VMEM)
    score_shape = (2, width // group, heads * group // width * residues, residues)
    return pl.pallas_call(
        attend_kernel,
        out_shape=jax.ShapeDtypeStruct(cells.shape, jnp.bfloat16),
        in_specs=[vmem] * 5,
        out_specs=vmem,
        scratch_shapes=[pltpu.VMEM(score_shape, jnp.float32)],
        compiler_params=pltpu.CompilerParams(vmem_limit_bytes=24 << 20),
        name="attend_rows",
    )(cells, weights, out_weight, vectors, bias)


def local(
    source_alignment_rows,
    pairs,
    chain_first_residue,
    gap_embedding,
    layer_norm_gain,
    layer_norm_bias,
    projection_weight,
    gate_bias_heads,
    pair_bias_logits,
    output_weight,
    output_bias,
):
    local_rows, local_columns, channels = source_alignment_rows.shape
    owners = lax.axis_size("rows")
    members = lax.axis_size("res")
    near, other, order = gather_bias(pair_bias_logits)
    blocks = [source_alignment_rows]
    for hop in range(1, owners):
        blocks.append(
            lax.ppermute(
                source_alignment_rows, "rows", [(i, (i + hop) % owners) for i in range(owners)]
            )
        )
    weights = turn_weights(projection_weight)
    arrived = []
    for part in range(parts):
        picked = pick(part, parts, pairs, chain_first_residue, gap_embedding, blocks, (weights,))
        arrived.append(lax.all_to_all(picked, "res", split_axis=0, concat_axis=0, tiled=True))
    bias, vectors = order_bias(
        near,
        other,
        order,
        (layer_norm_gain, layer_norm_bias, output_bias, gate_bias_heads),
        (weights, output_weight),
    )
    results = []
    for cells in arrived:
        part_rows = cells.shape[0]
        update = attend(
            cells.reshape(members, part_rows // members, local_columns, channels),
            weights,
            output_weight,
            vectors,
            bias,
        )
        update = update.reshape(part_rows, local_columns, channels)
        results.append(lax.all_to_all(update, "res", split_axis=0, concat_axis=0, tiled=True))
    return jnp.concatenate(results, axis=0)


def solution(mesh):
    return jax.shard_map(
        local,
        mesh=mesh,
        in_specs=(
            P("rows", "res", None),
            P(None, "rows"),
            P(),
            P(),
            P(),
            P(),
            P(),
            P(),
            P(None, "res", None),
            P(),
            P(),
        ),
        out_specs=P("rows", "res", None),
        check_vma=False,
    )
```

```python
import functools
import math

import jax
import jax.numpy as jnp
from jax import lax
from jax.experimental import pallas as pl
from jax.experimental.pallas import tpu as pltpu
from jax.sharding import PartitionSpec as P

norm_eps = 1e-05
log2e = math.log2(math.e)
cores = 2


def pick_kernel(owners, first_row, pairs_ref, first_ref, gap_ref, *refs):
    blocks, (out_ref, held, sems) = refs[:owners], refs[-3:]
    local_rows, local_columns, channels = blocks[0].shape
    part_rows = out_ref.shape[0]
    pieces = sems.shape[0]
    piece_rows = part_rows // pieces
    chains = first_ref.shape[0]
    shift = local_rows.bit_length() - 1
    assert local_rows == 1 << shift
    me = lax.axis_index("rows")
    start = lax.axis_index("res") * local_columns
    low, high = jnp.int32(0), jnp.int32(0)
    for k in range(1, chains):
        low += (first_ref[k] <= start).astype(jnp.int32)
        high += (first_ref[k] <= start + local_columns - 1).astype(jnp.int32)
    edge = first_ref[high] - start
    in_high = lax.broadcasted_iota(jnp.int32, (local_columns, channels), 0) >= edge
    gap = gap_ref[...].astype(jnp.float32).reshape(1, channels)
    gap = jnp.broadcast_to(gap, (local_columns, channels))
    names = [lax.rem(me - k + owners, owners) for k in range(owners)]

    def cells(row):
        owner = row >> shift
        within = row & (local_rows - 1)
        found = blocks[0][within].astype(jnp.float32)
        for k in range(1, owners):
            found = jnp.where(owner == names[k], blocks[k][within].astype(jnp.float32), found)
        return jnp.where(row >= 0, found, gap)

    def one_row(s, carry):
        row = first_row + s
        picked = jnp.where(in_high, cells(pairs_ref[high, row]), cells(pairs_ref[low, row]))
        held[s] = picked.astype(jnp.bfloat16)
        return carry

    copies = []
    for k in range(pieces):
        rows = pl.ds(k * piece_rows, piece_rows)
        lax.fori_loop(k * piece_rows, (k + 1) * piece_rows, one_row, 0, unroll=piece_rows)
        copies.append(pltpu.make_async_copy(held.at[rows], out_ref.at[rows], sems.at[k]))
        copies[-1].start()
    for copy in copies:
        copy.wait()


def pick(part, parts, pairs, chain_first_residue, gap, blocks, earlier):
    owners = len(blocks)
    local_rows, local_columns, channels = blocks[0].shape
    part_rows = local_rows // parts
    pieces = part_rows // 16
    smem = pl.BlockSpec(memory_space=pltpu.SMEM)
    vmem = pl.BlockSpec(memory_space=pltpu.VMEM)
    anywhere = pl.BlockSpec(memory_space=pl.ANY)
    block_bytes = local_rows * local_columns * channels * 2
    shape = (part_rows, local_columns, channels)
    return pl.pallas_call(
        functools.partial(pick_kernel, owners, part * part_rows),
        out_shape=jax.ShapeDtypeStruct(shape, jnp.bfloat16),
        in_specs=[smem, smem, vmem] + [vmem] * owners + [anywhere] * len(earlier),
        out_specs=anywhere,
        scratch_shapes=[pltpu.VMEM(shape, jnp.bfloat16), pltpu.SemaphoreType.DMA((pieces,))],
        compiler_params=pltpu.CompilerParams(vmem_limit_bytes=(owners + 4) * block_bytes),
        name="pick_joint",
    )(pairs, chain_first_residue, gap, *blocks, *earlier)


def bias_kernel(order, near_ref, far_ref, *refs):
    rows, gate_ref, (out_ref, vectors_ref, held) = refs[:3], refs[3], refs[-3:]
    me = lax.axis_index("res")
    half, heads, block, _ = near_ref.shape
    for place, flip in enumerate(order):
        source = near_ref if place < half else far_ref
        first = pl.multiple_of((me ^ flip) * block, block)
        held[:, pl.ds(first, block), :] = source[place % half].astype(jnp.float32)

    def one_head(h, carry):
        out_ref[h] = held[h].T * log2e
        return carry

    lax.fori_loop(0, heads, one_head, 0)
    width = gate_ref.shape[0]
    for place, ref in enumerate(rows):
        vectors_ref[place : place + 1] = ref[...].astype(jnp.float32).reshape(1, width)
    gate = gate_ref[...].astype(jnp.float32).reshape(1, width)
    vectors_ref[8:] = jnp.broadcast_to(gate, (width, width)).T


def gather_bias(shard):
    members = lax.axis_size("res")

    def swap(piece, flip):
        return lax.ppermute(piece, "res", [(i, i ^ flip) for i in range(members)])

    far, next_far = members // 2, members // 4
    shard = shard[None]
    pieces = [shard]
    order = [0]
    for flip in (far, next_far, far + next_far):
        pieces.append(swap(shard, flip))
        order.append(flip)
    flip = members // 8
    while flip > 1:
        pieces += [swap(piece, flip) for piece in pieces]
        order += [place ^ flip for place in order]
        flip //= 2
    near = jnp.concatenate(pieces, axis=0)
    return near, swap(near, 1), order + [place ^ 1 for place in order]


def order_bias(near, other, order, vectors, earlier):
    half, heads, block, keys = near.shape
    width = vectors[-1].shape[0]
    vmem = pl.BlockSpec(memory_space=pltpu.VMEM)
    anywhere = pl.BlockSpec(memory_space=pl.ANY)
    return pl.pallas_call(
        functools.partial(bias_kernel, order),
        out_shape=[
            jax.ShapeDtypeStruct((heads, keys, 2 * half * block), jnp.float32),
            jax.ShapeDtypeStruct((8 + width, width), jnp.float32),
        ],
        in_specs=[vmem] * (2 + len(vectors)) + [anywhere] * len(earlier),
        out_specs=[vmem] * 2,
        scratch_shapes=[pltpu.VMEM((heads, 2 * half * block, keys), jnp.float32)],
        compiler_params=pltpu.CompilerParams(vmem_limit_bytes=14 << 20),
        name="order_bias",
    )(near, other, *vectors, *earlier)


def weights_kernel(heads, weight_ref, weights_ref):
    width = weight_ref.shape[1] // 4
    depth = width // heads
    turned = weight_ref[...].T
    kinds = []
    for kind in range(4):
        rows = [turned[(h * 4 + kind) * depth : (h * 4 + kind + 1) * depth] for h in range(heads)]
        kinds.append(jnp.concatenate(rows, axis=0))
    for place, kind in enumerate((kinds[0], kinds[2], kinds[3], kinds[1].T)):
        weights_ref[place * width : (place + 1) * width] = kind


def turn_weights(projection_weight):
    channels, heads, four = projection_weight.shape
    width = heads * four // 4
    vmem = pl.BlockSpec(memory_space=pltpu.VMEM)
    return pl.pallas_call(
        functools.partial(weights_kernel, heads),
        out_shape=jax.ShapeDtypeStruct((4 * width, channels), jnp.bfloat16),
        in_specs=[vmem],
        out_specs=vmem,
        compiler_params=pltpu.CompilerParams(vmem_limit_bytes=8 << 20),
        name="turn_weights",
    )(projection_weight.reshape(channels, heads * four))


def attend_kernel(cells_ref, weights_ref, out_weight_ref, vectors_ref, bias_ref, *refs):
    out_refs, (staged_ref, scores_ref) = refs[:-2], refs[-2:]
    senders, rows, block, channels = cells_ref.shape
    me = lax.axis_index("res")
    residues = senders * block
    heads = bias_ref.shape[0]
    width = weights_ref.shape[0] // 4
    depth = width // heads
    ones = jnp.ones((16, residues), jnp.bfloat16)
    group = min(128, width)
    head_of = lax.broadcasted_iota(jnp.int32, (1, group), 1) // depth
    masks = [(head_of == h).astype(jnp.bfloat16) for h in range(group // depth)]

    def begin(r):
        wide = cells_ref[:, r].reshape(residues, channels).astype(jnp.float32)
        center = jnp.mean(wide, axis=-1, keepdims=True)
        wide = wide - center
        spread = jnp.mean(jnp.square(wide), axis=-1, keepdims=True)
        normed = wide * lax.rsqrt(spread + norm_eps) * vectors_ref[0:1] + vectors_ref[1:2]
        normed = normed.astype(jnp.bfloat16)
        keys = jnp.dot(
            normed, weights_ref[3 * width :], preferred_element_type=jnp.float32
        )
        rest = lax.dot_general(
            weights_ref[: 3 * width], normed, (((1,), (1,)), ((), ())),
            preferred_element_type=jnp.float32,
        )
        queries = (rest[:width] * (depth**-0.5 * log2e)).astype(jnp.bfloat16)
        values = rest[width : 2 * width].astype(jnp.bfloat16)
        keys = keys.astype(jnp.bfloat16)
        for k in range(width // group):
            lanes = slice(k * group, (k + 1) * group)
            stack = jnp.concatenate([keys[:, lanes] * mask for mask in masks], axis=0)
            scores_ref[r % 2, k] = jnp.dot(
                stack, queries[lanes], preferred_element_type=jnp.float32
            )
        gates = 0.5 + 0.5 * jnp.tanh(0.5 * (rest[2 * width :] + vectors_ref[8:]))
        return values, gates

    def weigh(r, h):
        values, gates = begun[r]
        low, high = h * depth, (h + 1) * depth
        first = low % group // depth * residues
        scores = scores_ref[r % 2, low // group, first : first + residues] + bias_ref[h]
        highest = jnp.max(scores, axis=0, keepdims=True)
        lifted = jnp.exp2(scores - highest).astype(jnp.bfloat16)
        left = jnp.concatenate([values[low:high], ones], axis=0)
        summed = jnp.dot(left, lifted, preferred_element_type=jnp.float32)
        inverse = 1.0 / summed[depth : depth + 1]
        return (summed[:depth] * (gates[low:high] * inverse)).astype(jnp.bfloat16)

    def finish(r, heads_out):
        attended = jnp.concatenate(heads_out, axis=0).T
        update = jnp.dot(attended, out_weight_ref[...], preferred_element_type=jnp.float32)
        update = (update + vectors_ref[2:3]).astype(jnp.bfloat16)
        staged_ref[...] = update.reshape(senders, block, channels)
        for flip in range(senders):
            out_refs[flip // cores][flip % cores, r] = staged_ref[me ^ flip]

    begun = {0: begin(0)}
    done = {r: [] for r in range(rows)}
    for r in range(rows):
        for h in range(heads):
            if h == heads // 2 and r + 1 < rows:
                begun[r + 1] = begin(r + 1)
            done[r].append(weigh(r, h))
            if h == 0 and r:
                finish(r - 1, done[r - 1])
    finish(rows - 1, done[rows - 1])


def attend(cells, weights, out_weight, vectors, bias):
    heads, residues, _ = bias.shape
    senders, rows, block, channels = cells.shape
    width = weights.shape[0] // 4
    group = min(128, width)
    vmem = pl.BlockSpec(memory_space=pltpu.VMEM)
    score_shape = (2, width // group, heads * group // width * residues, residues)
    piece = jax.ShapeDtypeStruct((cores, rows, block, channels), jnp.bfloat16)
    return pl.pallas_call(
        attend_kernel,
        out_shape=[piece] * (senders // cores),
        in_specs=[vmem] * 5,
        out_specs=[vmem] * (senders // cores),
        scratch_shapes=[
            pltpu.VMEM((senders, block, channels), jnp.bfloat16),
            pltpu.VMEM(score_shape, jnp.float32),
        ],
        compiler_params=pltpu.CompilerParams(vmem_limit_bytes=24 << 20),
        name="attend_rows",
    )(cells, weights, out_weight, vectors, bias)


def swap(array, flip):
    members = lax.axis_size("res")
    return lax.ppermute(array, "res", [(i, i ^ flip) for i in range(members)])


def spread(pieces):
    half = len(pieces) // 2
    order = [1, *range(half, len(pieces)), *range(2, half), 0]
    arrived = [swap(pieces[chip], chip * cores) if chip else pieces[0] for chip in order]
    return order, arrived, swap(jnp.stack([piece[1] for piece in arrived]), 1)


def place_kernel(order, *refs):
    piece_refs, (other_ref, out_ref, sems) = refs[:-3], refs[-3:]
    me = lax.axis_index("res")
    rows = other_ref.shape[1]
    copies = []
    for k, chip in enumerate(order):
        for core, source in enumerate((piece_refs[k].at[0], other_ref.at[k])):
            first = (me ^ (chip * cores + core)) * rows
            target = out_ref.at[pl.ds(first, rows)]
            copies.append(pltpu.make_async_copy(source, target, sems.at[len(copies)]))
    for copy in copies:
        copy.start()
    for copy in copies:
        copy.wait()


def place(order, pieces, other, shape):
    vmem = pl.BlockSpec(memory_space=pltpu.VMEM)
    return pl.pallas_call(
        functools.partial(place_kernel, order),
        out_shape=jax.ShapeDtypeStruct(shape, jnp.bfloat16),
        in_specs=[vmem] * (len(pieces) + 1),
        out_specs=pl.BlockSpec(memory_space=pl.ANY),
        scratch_shapes=[pltpu.SemaphoreType.DMA((cores * len(pieces),))],
        compiler_params=pltpu.CompilerParams(vmem_limit_bytes=8 << 20),
        name="place_rows",
    )(*pieces, other)


def local(
    source_alignment_rows,
    pairs,
    chain_first_residue,
    gap_embedding,
    layer_norm_gain,
    layer_norm_bias,
    projection_weight,
    gate_bias_heads,
    pair_bias_logits,
    output_weight,
    output_bias,
):
    local_rows, local_columns, channels = source_alignment_rows.shape
    owners = lax.axis_size("rows")
    members = lax.axis_size("res")
    near, other, order = gather_bias(pair_bias_logits)
    blocks = [source_alignment_rows]
    for hop in range(1, owners):
        blocks.append(
            lax.ppermute(
                source_alignment_rows, "rows", [(i, (i + hop) % owners) for i in range(owners)]
            )
        )
    weights = turn_weights(projection_weight)
    joint = pick(0, 1, pairs, chain_first_residue, gap_embedding, blocks, (weights,))
    cells = lax.all_to_all(joint, "res", split_axis=0, concat_axis=0, tiled=True)
    bias, vectors = order_bias(
        near,
        other,
        order,
        (layer_norm_gain, layer_norm_bias, output_bias, gate_bias_heads),
        (weights, output_weight),
    )
    cells = cells.reshape(members, local_rows // members, local_columns, channels)
    arrived = spread(attend(cells, weights, output_weight, vectors, bias))
    return place(*arrived, (local_rows, local_columns, channels))


def solution(mesh):
    return jax.shard_map(
        local,
        mesh=mesh,
        in_specs=(
            P("rows", "res", None),
            P(None, "rows"),
            P(),
            P(),
            P(),
            P(),
            P(),
            P(),
            P(None, "res", None),
            P(),
            P(),
        ),
        out_specs=P("rows", "res", None),
        check_vma=False,
    )
```

```python
import functools
import math

import jax
import jax.numpy as jnp
from jax import lax
from jax.experimental import pallas as pl
from jax.experimental.pallas import tpu as pltpu
from jax.sharding import PartitionSpec as P

norm_eps = 1e-05
log2e = math.log2(math.e)
cores = 2


def pick_kernel(owners, first_row, pairs_ref, first_ref, gap_ref, *refs):
    blocks, (out_ref, held, sems) = refs[:owners], refs[-3:]
    local_rows, local_columns, channels = blocks[0].shape
    part_rows = out_ref.shape[0]
    pieces = sems.shape[0]
    piece_rows = part_rows // pieces
    chains = first_ref.shape[0]
    shift = local_rows.bit_length() - 1
    assert local_rows == 1 << shift
    me = lax.axis_index("rows")
    start = lax.axis_index("res") * local_columns
    low, high = jnp.int32(0), jnp.int32(0)
    for k in range(1, chains):
        low += (first_ref[k] <= start).astype(jnp.int32)
        high += (first_ref[k] <= start + local_columns - 1).astype(jnp.int32)
    edge = first_ref[high] - start
    in_high = lax.broadcasted_iota(jnp.int32, (local_columns, channels), 0) >= edge
    gap = gap_ref[...].astype(jnp.float32).reshape(1, channels)
    gap = jnp.broadcast_to(gap, (local_columns, channels))
    names = [lax.rem(me - k + owners, owners) for k in range(owners)]

    def cells(row):
        owner = row >> shift
        within = row & (local_rows - 1)
        found = blocks[0][within].astype(jnp.float32)
        for k in range(1, owners):
            found = jnp.where(owner == names[k], blocks[k][within].astype(jnp.float32), found)
        return jnp.where(row >= 0, found, gap)

    def one_row(s, carry):
        row = first_row + s
        picked = jnp.where(in_high, cells(pairs_ref[high, row]), cells(pairs_ref[low, row]))
        held[s] = picked.astype(jnp.bfloat16)
        return carry

    copies = []
    for k in range(pieces):
        rows = pl.ds(k * piece_rows, piece_rows)
        lax.fori_loop(k * piece_rows, (k + 1) * piece_rows, one_row, 0, unroll=piece_rows)
        copies.append(pltpu.make_async_copy(held.at[rows], out_ref.at[rows], sems.at[k]))
        copies[-1].start()
    for copy in copies:
        copy.wait()


def pick(part, parts, pairs, chain_first_residue, gap, blocks, earlier):
    owners = len(blocks)
    local_rows, local_columns, channels = blocks[0].shape
    part_rows = local_rows // parts
    pieces = part_rows // 16
    smem = pl.BlockSpec(memory_space=pltpu.SMEM)
    vmem = pl.BlockSpec(memory_space=pltpu.VMEM)
    anywhere = pl.BlockSpec(memory_space=pl.ANY)
    block_bytes = local_rows * local_columns * channels * 2
    shape = (part_rows, local_columns, channels)
    return pl.pallas_call(
        functools.partial(pick_kernel, owners, part * part_rows),
        out_shape=jax.ShapeDtypeStruct(shape, jnp.bfloat16),
        in_specs=[smem, smem, vmem] + [vmem] * owners + [anywhere] * len(earlier),
        out_specs=anywhere,
        scratch_shapes=[pltpu.VMEM(shape, jnp.bfloat16), pltpu.SemaphoreType.DMA((pieces,))],
        compiler_params=pltpu.CompilerParams(vmem_limit_bytes=(owners + 4) * block_bytes),
        name="pick_joint",
    )(pairs, chain_first_residue, gap, *blocks, *earlier)


def bias_kernel(order, near_ref, far_ref, *refs):
    rows, gate_ref, (out_ref, vectors_ref, held) = refs[:3], refs[3], refs[-3:]
    me = lax.axis_index("res")
    half, heads, block, _ = near_ref.shape
    for place, flip in enumerate(order):
        source = near_ref if place < half else far_ref
        first = pl.multiple_of((me ^ flip) * block, block)
        held[:, pl.ds(first, block), :] = source[place % half].astype(jnp.float32)

    def one_head(h, carry):
        out_ref[h] = held[h].T * log2e
        return carry

    lax.fori_loop(0, heads, one_head, 0)
    width = gate_ref.shape[0]
    for place, ref in enumerate(rows):
        vectors_ref[place : place + 1] = ref[...].astype(jnp.float32).reshape(1, width)
    gate = gate_ref[...].astype(jnp.float32).reshape(1, width)
    vectors_ref[8:] = jnp.broadcast_to(gate, (width, width)).T


def gather_bias(shard):
    members = lax.axis_size("res")

    def swap(piece, flip):
        return lax.ppermute(piece, "res", [(i, i ^ flip) for i in range(members)])

    far, next_far = members // 2, members // 4
    shard = shard[None]
    pieces = [shard]
    order = [0]
    for flip in (far, next_far, far + next_far):
        pieces.append(swap(shard, flip))
        order.append(flip)
    flip = members // 8
    while flip > 1:
        pieces += [swap(piece, flip) for piece in pieces]
        order += [place ^ flip for place in order]
        flip //= 2
    near = jnp.concatenate(pieces, axis=0)
    return near, swap(near, 1), order + [place ^ 1 for place in order]


def order_bias(near, other, order, vectors, earlier):
    half, heads, block, keys = near.shape
    width = vectors[-1].shape[0]
    vmem = pl.BlockSpec(memory_space=pltpu.VMEM)
    anywhere = pl.BlockSpec(memory_space=pl.ANY)
    return pl.pallas_call(
        functools.partial(bias_kernel, order),
        out_shape=[
            jax.ShapeDtypeStruct((heads, keys, 2 * half * block), jnp.float32),
            jax.ShapeDtypeStruct((8 + width, width), jnp.float32),
        ],
        in_specs=[vmem] * (2 + len(vectors)) + [anywhere] * len(earlier),
        out_specs=[vmem] * 2,
        scratch_shapes=[pltpu.VMEM((heads, 2 * half * block, keys), jnp.float32)],
        compiler_params=pltpu.CompilerParams(vmem_limit_bytes=14 << 20),
        name="order_bias",
    )(near, other, *vectors, *earlier)


def weights_kernel(heads, weight_ref, weights_ref):
    width = weight_ref.shape[1] // 4
    depth = width // heads
    turned = weight_ref[...].T
    kinds = []
    for kind in range(4):
        rows = [turned[(h * 4 + kind) * depth : (h * 4 + kind + 1) * depth] for h in range(heads)]
        kinds.append(jnp.concatenate(rows, axis=0))
    for place, kind in enumerate((kinds[0], kinds[2], kinds[3], kinds[1].T)):
        weights_ref[place * width : (place + 1) * width] = kind


def turn_weights(projection_weight):
    channels, heads, four = projection_weight.shape
    width = heads * four // 4
    vmem = pl.BlockSpec(memory_space=pltpu.VMEM)
    return pl.pallas_call(
        functools.partial(weights_kernel, heads),
        out_shape=jax.ShapeDtypeStruct((4 * width, channels), jnp.bfloat16),
        in_specs=[vmem],
        out_specs=vmem,
        compiler_params=pltpu.CompilerParams(vmem_limit_bytes=8 << 20),
        name="turn_weights",
    )(projection_weight.reshape(channels, heads * four))


def attend_kernel(cells_ref, weights_ref, out_weight_ref, vectors_ref, bias_ref, *refs):
    out_refs, (staged_ref, scores_ref) = refs[:-2], refs[-2:]
    senders, rows, block, channels = cells_ref.shape
    me = lax.axis_index("res")
    residues = senders * block
    heads = bias_ref.shape[0]
    width = weights_ref.shape[0] // 4
    depth = width // heads
    ones = jnp.ones((16, residues), jnp.bfloat16)
    group = min(128, width)
    head_of = lax.broadcasted_iota(jnp.int32, (1, group), 1) // depth
    masks = [(head_of == h).astype(jnp.bfloat16) for h in range(group // depth)]

    def begin(r):
        wide = cells_ref[:, r].reshape(residues, channels).astype(jnp.float32)
        center = jnp.mean(wide, axis=-1, keepdims=True)
        wide = wide - center
        spread = jnp.mean(jnp.square(wide), axis=-1, keepdims=True)
        normed = wide * lax.rsqrt(spread + norm_eps) * vectors_ref[0:1] + vectors_ref[1:2]
        normed = normed.astype(jnp.bfloat16)
        keys = jnp.dot(
            normed, weights_ref[3 * width :], preferred_element_type=jnp.float32
        )
        rest = lax.dot_general(
            weights_ref[: 3 * width], normed, (((1,), (1,)), ((), ())),
            preferred_element_type=jnp.float32,
        )
        queries = (rest[:width] * (depth**-0.5 * log2e)).astype(jnp.bfloat16)
        values = rest[width : 2 * width].astype(jnp.bfloat16)
        keys = keys.astype(jnp.bfloat16)
        for k in range(width // group):
            lanes = slice(k * group, (k + 1) * group)
            stack = jnp.concatenate([keys[:, lanes] * mask for mask in masks], axis=0)
            scores_ref[r % 2, k] = jnp.dot(
                stack, queries[lanes], preferred_element_type=jnp.float32
            )
        gates = 0.5 + 0.5 * jnp.tanh(0.5 * (rest[2 * width :] + vectors_ref[8:]))
        return values, gates

    def weigh(r, h):
        values, gates = begun[r]
        low, high = h * depth, (h + 1) * depth
        first = low % group // depth * residues
        scores = scores_ref[r % 2, low // group, first : first + residues] + bias_ref[h]
        highest = jnp.max(scores, axis=0, keepdims=True)
        lifted = jnp.exp2(scores - highest).astype(jnp.bfloat16)
        left = jnp.concatenate([values[low:high], ones], axis=0)
        summed = jnp.dot(left, lifted, preferred_element_type=jnp.float32)
        inverse = 1.0 / summed[depth : depth + 1]
        return (summed[:depth] * (gates[low:high] * inverse)).astype(jnp.bfloat16)

    def finish(r, heads_out):
        attended = jnp.concatenate(heads_out, axis=0).T
        update = jnp.dot(attended, out_weight_ref[...], preferred_element_type=jnp.float32)
        update = (update + vectors_ref[2:3]).astype(jnp.bfloat16)
        staged_ref[...] = update.reshape(senders, block, channels)
        for flip in range(senders):
            out_refs[flip // cores][flip % cores, r] = staged_ref[me ^ flip]

    begun = {0: begin(0)}
    done = {r: [] for r in range(rows)}
    for r in range(rows):
        for h in range(heads):
            if h == heads // 2 and r + 1 < rows:
                begun[r + 1] = begin(r + 1)
            done[r].append(weigh(r, h))
            if h == 0 and r:
                finish(r - 1, done[r - 1])
    finish(rows - 1, done[rows - 1])


def attend(cells, weights, out_weight, vectors, bias):
    heads, residues, _ = bias.shape
    senders, rows, block, channels = cells.shape
    width = weights.shape[0] // 4
    group = min(128, width)
    vmem = pl.BlockSpec(memory_space=pltpu.VMEM)
    score_shape = (2, width // group, heads * group // width * residues, residues)
    piece = jax.ShapeDtypeStruct((cores, rows, block, channels), jnp.bfloat16)
    return pl.pallas_call(
        attend_kernel,
        out_shape=[piece] * (senders // cores),
        in_specs=[vmem] * 5,
        out_specs=[vmem] * (senders // cores),
        scratch_shapes=[
            pltpu.VMEM((senders, block, channels), jnp.bfloat16),
            pltpu.VMEM(score_shape, jnp.float32),
        ],
        compiler_params=pltpu.CompilerParams(vmem_limit_bytes=24 << 20),
        name="attend_rows",
    )(cells, weights, out_weight, vectors, bias)


def swap(array, flip):
    members = lax.axis_size("res")
    return lax.ppermute(array, "res", [(i, i ^ flip) for i in range(members)])


def spread(pieces):
    half = len(pieces) // 2
    line = half // 2
    order = [line, *range(half, 2 * half), *range(line + 1, half), *range(1, line), 0]
    arrived = [swap(pieces[chip], chip * cores) if chip else pieces[0] for chip in order]
    return order, arrived, swap(jnp.stack([piece[1] for piece in arrived]), 1)


def place_kernel(order, *refs):
    piece_refs, (other_ref, out_ref, sems) = refs[:-3], refs[-3:]
    me = lax.axis_index("res")
    rows = other_ref.shape[1]
    copies = []
    for k, chip in enumerate(order):
        for core, source in enumerate((piece_refs[k].at[0], other_ref.at[k])):
            first = (me ^ (chip * cores + core)) * rows
            target = out_ref.at[pl.ds(first, rows)]
            copies.append(pltpu.make_async_copy(source, target, sems.at[len(copies)]))
    for copy in copies:
        copy.start()
    for copy in copies:
        copy.wait()


def place(order, pieces, other, shape):
    vmem = pl.BlockSpec(memory_space=pltpu.VMEM)
    return pl.pallas_call(
        functools.partial(place_kernel, order),
        out_shape=jax.ShapeDtypeStruct(shape, jnp.bfloat16),
        in_specs=[vmem] * (len(pieces) + 1),
        out_specs=pl.BlockSpec(memory_space=pl.ANY),
        scratch_shapes=[pltpu.SemaphoreType.DMA((cores * len(pieces),))],
        compiler_params=pltpu.CompilerParams(vmem_limit_bytes=8 << 20),
        name="place_rows",
    )(*pieces, other)


def local(
    source_alignment_rows,
    pairs,
    chain_first_residue,
    gap_embedding,
    layer_norm_gain,
    layer_norm_bias,
    projection_weight,
    gate_bias_heads,
    pair_bias_logits,
    output_weight,
    output_bias,
):
    local_rows, local_columns, channels = source_alignment_rows.shape
    owners = lax.axis_size("rows")
    members = lax.axis_size("res")
    near, other, order = gather_bias(pair_bias_logits)
    blocks = [source_alignment_rows]
    for hop in range(1, owners):
        blocks.append(
            lax.ppermute(
                source_alignment_rows, "rows", [(i, (i + hop) % owners) for i in range(owners)]
            )
        )
    weights = turn_weights(projection_weight)
    joint = pick(0, 1, pairs, chain_first_residue, gap_embedding, blocks, (weights,))
    cells = lax.all_to_all(joint, "res", split_axis=0, concat_axis=0, tiled=True)
    bias, vectors = order_bias(
        near,
        other,
        order,
        (layer_norm_gain, layer_norm_bias, output_bias, gate_bias_heads),
        (weights, output_weight),
    )
    cells = cells.reshape(members, local_rows // members, local_columns, channels)
    arrived = spread(attend(cells, weights, output_weight, vectors, bias))
    return place(*arrived, (local_rows, local_columns, channels))


def solution(mesh):
    return jax.shard_map(
        local,
        mesh=mesh,
        in_specs=(
            P("rows", "res", None),
            P(None, "rows"),
            P(),
            P(),
            P(),
            P(),
            P(),
            P(),
            P(None, "res", None),
            P(),
            P(),
        ),
        out_specs=P("rows", "res", None),
        check_vma=False,
    )
```

```python
import functools

import jax
import jax.numpy as jnp
from jax import lax
from jax.experimental import pallas as pl
from jax.experimental.pallas import tpu as pltpu
from jax.sharding import PartitionSpec as P

norm_eps = 1e-05
cores = 2


def pick_kernel(owners, pairs_ref, first_ref, gap_ref, *refs):
    blocks, (out_ref, held, sems) = refs[:owners], refs[-3:]
    local_rows, local_columns, channels = blocks[0].shape
    part_rows = out_ref.shape[0]
    pieces = sems.shape[0]
    piece_rows = part_rows // pieces
    chains = first_ref.shape[0]
    shift = local_rows.bit_length() - 1
    assert local_rows == 1 << shift
    me = lax.axis_index("rows")
    start = lax.axis_index("res") * local_columns
    low, high = jnp.int32(0), jnp.int32(0)
    for k in range(1, chains):
        low += (first_ref[k] <= start).astype(jnp.int32)
        high += (first_ref[k] <= start + local_columns - 1).astype(jnp.int32)
    edge = first_ref[high] - start
    in_high = lax.broadcasted_iota(jnp.int32, (local_columns, channels), 0) >= edge
    gap = gap_ref[...].astype(jnp.float32).reshape(1, channels)
    gap = jnp.broadcast_to(gap, (local_columns, channels))
    names = [lax.rem(me - k + owners, owners) for k in range(owners)]

    def cells(row):
        owner = row >> shift
        within = row & (local_rows - 1)
        found = blocks[0][within].astype(jnp.float32)
        for k in range(1, owners):
            found = jnp.where(owner == names[k], blocks[k][within].astype(jnp.float32), found)
        return jnp.where(row >= 0, found, gap)

    copies = []
    for k in range(pieces):
        rows = pl.ds(k * piece_rows, piece_rows)
        for row in range(k * piece_rows, (k + 1) * piece_rows):
            both = jnp.where(in_high, cells(pairs_ref[high, row]), cells(pairs_ref[low, row]))
            held[row] = both.astype(jnp.bfloat16)
        copies.append(pltpu.make_async_copy(held.at[rows], out_ref.at[rows], sems.at[k]))
        copies[-1].start()
    for copy in copies:
        copy.wait()


def pick(pairs, chain_first_residue, gap, blocks, earlier):
    owners = len(blocks)
    local_rows, local_columns, channels = blocks[0].shape
    pieces = 2
    smem = pl.BlockSpec(memory_space=pltpu.SMEM)
    vmem = pl.BlockSpec(memory_space=pltpu.VMEM)
    anywhere = pl.BlockSpec(memory_space=pl.ANY)
    block_bytes = local_rows * local_columns * channels * 2
    shape = blocks[0].shape
    return pl.pallas_call(
        functools.partial(pick_kernel, owners),
        out_shape=jax.ShapeDtypeStruct(shape, jnp.bfloat16),
        in_specs=[smem, smem, vmem] + [vmem] * owners + [anywhere] * len(earlier),
        out_specs=anywhere,
        scratch_shapes=[pltpu.VMEM(shape, jnp.bfloat16), pltpu.SemaphoreType.DMA((pieces,))],
        compiler_params=pltpu.CompilerParams(vmem_limit_bytes=(owners + 4) * block_bytes),
        name="pick_joint",
    )(pairs, chain_first_residue, gap, *blocks, *earlier)


def bias_kernel(order, near_ref, far_ref, *refs):
    rows, gate_ref, (out_ref, vectors_ref, held) = refs[:3], refs[3], refs[-3:]
    me = lax.axis_index("res")
    half, heads, block, _ = near_ref.shape
    for place, flip in enumerate(order):
        source = near_ref if place < half else far_ref
        first = pl.multiple_of((me ^ flip) * block, block)
        held[:, pl.ds(first, block), :] = source[place % half].astype(jnp.float32)

    def one_head(h, carry):
        out_ref[h] = held[h].T
        return carry

    lax.fori_loop(0, heads, one_head, 0)
    width = gate_ref.shape[0]
    for place, ref in enumerate(rows):
        vectors_ref[place : place + 1] = ref[...].astype(jnp.float32).reshape(1, width)
    gate = gate_ref[...].astype(jnp.float32).reshape(1, width)
    vectors_ref[8:] = jnp.broadcast_to(gate, (width, width)).T


def gather_bias(shard):
    members = lax.axis_size("res")

    def swap(piece, flip):
        return lax.ppermute(piece, "res", [(i, i ^ flip) for i in range(members)])

    far, next_far = members // 2, members // 4
    shard = shard[None]
    pieces = [shard]
    order = [0]
    for flip in (far, next_far, far + next_far):
        pieces.append(swap(shard, flip))
        order.append(flip)
    flip = members // 8
    while flip > 1:
        pieces += [swap(piece, flip) for piece in pieces]
        order += [place ^ flip for place in order]
        flip //= 2
    near = jnp.concatenate(pieces, axis=0)
    return near, swap(near, 1), order + [place ^ 1 for place in order]


def order_bias(near, other, order, vectors, earlier):
    half, heads, block, keys = near.shape
    width = vectors[-1].shape[0]
    vmem = pl.BlockSpec(memory_space=pltpu.VMEM)
    anywhere = pl.BlockSpec(memory_space=pl.ANY)
    return pl.pallas_call(
        functools.partial(bias_kernel, order),
        out_shape=[
            jax.ShapeDtypeStruct((heads, keys, 2 * half * block), jnp.float32),
            jax.ShapeDtypeStruct((8 + width, width), jnp.float32),
        ],
        in_specs=[vmem] * (2 + len(vectors)) + [anywhere] * len(earlier),
        out_specs=[vmem] * 2,
        scratch_shapes=[pltpu.VMEM((heads, 2 * half * block, keys), jnp.float32)],
        compiler_params=pltpu.CompilerParams(vmem_limit_bytes=14 << 20),
        name="order_bias",
    )(near, other, *vectors, *earlier)


def weights_kernel(heads, weight_ref, weights_ref):
    width = weight_ref.shape[1] // 4
    depth = width // heads
    turned = weight_ref[...].T
    kinds = []
    for kind in range(4):
        rows = [turned[(h * 4 + kind) * depth : (h * 4 + kind + 1) * depth] for h in range(heads)]
        kinds.append(jnp.concatenate(rows, axis=0))
    for place, kind in enumerate((kinds[0], kinds[2], kinds[3], kinds[1].T)):
        weights_ref[place * width : (place + 1) * width] = kind


def turn_weights(projection_weight):
    channels, heads, four = projection_weight.shape
    width = heads * four // 4
    vmem = pl.BlockSpec(memory_space=pltpu.VMEM)
    return pl.pallas_call(
        functools.partial(weights_kernel, heads),
        out_shape=jax.ShapeDtypeStruct((4 * width, channels), jnp.bfloat16),
        in_specs=[vmem],
        out_specs=vmem,
        compiler_params=pltpu.CompilerParams(vmem_limit_bytes=8 << 20),
        name="turn_weights",
    )(projection_weight.reshape(channels, heads * four))


def attend_kernel(cells_ref, weights_ref, out_weight_ref, vectors_ref, bias_ref, *refs):
    near_refs, far_refs, (staged_ref, scores_ref) = refs[:2], refs[2:-2], refs[-2:]
    senders, rows, block, channels = cells_ref.shape
    me = lax.axis_index("res")
    residues = senders * block
    heads = bias_ref.shape[0]
    width = weights_ref.shape[0] // 4
    depth = width // heads
    ones = jnp.ones((16, residues), jnp.bfloat16)
    group = min(128, width)
    head_of = lax.broadcasted_iota(jnp.int32, (1, group), 1) // depth
    masks = [(head_of == h).astype(jnp.bfloat16) for h in range(group // depth)]

    def begin(r):
        wide = cells_ref[:, r].reshape(residues, channels).astype(jnp.float32)
        center = jnp.mean(wide, axis=-1, keepdims=True)
        wide = wide - center
        spread = jnp.mean(jnp.square(wide), axis=-1, keepdims=True)
        normed = wide * lax.rsqrt(spread + norm_eps) * vectors_ref[0:1] + vectors_ref[1:2]
        normed = normed.astype(jnp.bfloat16)
        keys = jnp.dot(
            normed, weights_ref[3 * width :], preferred_element_type=jnp.float32
        )
        rest = lax.dot_general(
            weights_ref[: 3 * width], normed, (((1,), (1,)), ((), ())),
            preferred_element_type=jnp.float32,
        )
        queries = (rest[:width] * depth**-0.5).astype(jnp.bfloat16)
        values = rest[width : 2 * width].astype(jnp.bfloat16)
        keys = keys.astype(jnp.bfloat16)
        for k in range(width // group):
            lanes = slice(k * group, (k + 1) * group)
            stack = jnp.concatenate([keys[:, lanes] * mask for mask in masks], axis=0)
            scores_ref[r % 2, k] = jnp.dot(
                stack, queries[lanes], preferred_element_type=jnp.float32
            )
        gates = 0.5 + 0.5 * jnp.tanh(0.5 * (rest[2 * width :] + vectors_ref[8:]))
        return values, gates

    def weigh(r, h):
        values, gates = begun[r]
        low, high = h * depth, (h + 1) * depth
        first = low % group // depth * residues
        scores = scores_ref[r % 2, low // group, first : first + residues] + bias_ref[h]
        highest = jnp.max(scores, axis=0, keepdims=True)
        lifted = jnp.exp(scores - highest).astype(jnp.bfloat16)
        left = jnp.concatenate([values[low:high], ones], axis=0)
        summed = jnp.dot(left, lifted, preferred_element_type=jnp.float32)
        inverse = 1.0 / summed[depth : depth + 1]
        return (summed[:depth] * (gates[low:high] * inverse)).astype(jnp.bfloat16)

    def finish(r, heads_out):
        attended = jnp.concatenate(heads_out, axis=0).T
        update = jnp.dot(attended, out_weight_ref[...], preferred_element_type=jnp.float32)
        update = (update + vectors_ref[2:3]).astype(jnp.bfloat16)
        staged_ref[...] = update.reshape(senders, block, channels)
        for flip in range(senders):
            chip, core = flip // cores, flip % cores
            if chip < 4:
                near_refs[chip // 2][chip % 2, core, r] = staged_ref[me ^ flip]
            else:
                far_refs[chip - 4][core, r] = staged_ref[me ^ flip]

    begun = {0: begin(0)}
    done = {r: [] for r in range(rows)}
    for r in range(rows):
        for h in range(heads):
            if h == heads // 2 and r + 1 < rows:
                begun[r + 1] = begin(r + 1)
            done[r].append(weigh(r, h))
            if h == 0 and r:
                finish(r - 1, done[r - 1])
    finish(rows - 1, done[rows - 1])


def attend(cells, weights, out_weight, vectors, bias):
    heads, residues, _ = bias.shape
    senders, rows, block, channels = cells.shape
    width = weights.shape[0] // 4
    group = min(128, width)
    vmem = pl.BlockSpec(memory_space=pltpu.VMEM)
    score_shape = (2, width // group, heads * group // width * residues, residues)
    one = (cores, rows, block, channels)
    shapes = [(2, *one)] * 2 + [one] * (senders // cores - 4)
    return pl.pallas_call(
        attend_kernel,
        out_shape=[jax.ShapeDtypeStruct(shape, jnp.bfloat16) for shape in shapes],
        in_specs=[vmem] * 5,
        out_specs=[vmem] * len(shapes),
        scratch_shapes=[
            pltpu.VMEM((senders, block, channels), jnp.bfloat16),
            pltpu.VMEM(score_shape, jnp.float32),
        ],
        compiler_params=pltpu.CompilerParams(vmem_limit_bytes=24 << 20),
        name="attend_rows",
    )(cells, weights, out_weight, vectors, bias)


def swap(array, flip):
    members = lax.axis_size("res")
    return lax.ppermute(array, "res", [(i, i ^ flip) for i in range(members)])


def spread(pieces):
    here, there, far = pieces[0], pieces[1], pieces[2:]
    far = [swap(piece, (4 + k) * cores) for k, piece in enumerate(far)]
    there = swap(there, 2 * cores)
    hop = swap(jnp.stack([here[1], there[1]]), cores)
    middle = len(far) // 2
    arrived = [(4 + k, far[k]) for k in range(middle)] + [(2, there[0])]
    arrived += [(4 + k, far[k]) for k in range(middle, len(far))]
    arrived += [(1, hop[0]), (3, hop[1]), (0, here[0])]
    other = swap(jnp.stack([blocks[1] for _, blocks in arrived]), 1)
    return [chip for chip, _ in arrived], far, there, hop, here, other


def place_kernel(order, *refs):
    far_refs, (there_ref, hop_ref, here_ref, other_ref, out_ref, sems) = refs[:-6], refs[-6:]
    me = lax.axis_index("res")
    rows = other_ref.shape[1]
    near = [here_ref.at[0, 0], hop_ref.at[0, 0], there_ref.at[0, 0], hop_ref.at[1, 0]]
    copies = []
    for k, chip in enumerate(order):
        same = near[chip] if chip < 4 else far_refs[chip - 4].at[0]
        for core, source in enumerate((same, other_ref.at[k])):
            first = (me ^ (chip * cores + core)) * rows
            target = out_ref.at[pl.ds(first, rows)]
            copies.append(pltpu.make_async_copy(source, target, sems.at[len(copies)]))
    for copy in copies:
        copy.start()
    for copy in copies:
        copy.wait()


def place(order, far, there, hop, here, other, shape):
    vmem = pl.BlockSpec(memory_space=pltpu.VMEM)
    return pl.pallas_call(
        functools.partial(place_kernel, order),
        out_shape=jax.ShapeDtypeStruct(shape, jnp.bfloat16),
        in_specs=[vmem] * (len(far) + 4),
        out_specs=pl.BlockSpec(memory_space=pl.ANY),
        scratch_shapes=[pltpu.SemaphoreType.DMA((cores * len(order),))],
        compiler_params=pltpu.CompilerParams(vmem_limit_bytes=8 << 20),
        name="place_rows",
    )(*far, there, hop, here, other)


def local(
    source_alignment_rows,
    pairs,
    chain_first_residue,
    gap_embedding,
    layer_norm_gain,
    layer_norm_bias,
    projection_weight,
    gate_bias_heads,
    pair_bias_logits,
    output_weight,
    output_bias,
):
    local_rows, local_columns, channels = source_alignment_rows.shape
    owners = lax.axis_size("rows")
    members = lax.axis_size("res")
    near, other, order = gather_bias(pair_bias_logits)
    blocks = [source_alignment_rows]
    for hop in range(1, owners):
        blocks.append(
            lax.ppermute(
                source_alignment_rows, "rows", [(i, (i + hop) % owners) for i in range(owners)]
            )
        )
    weights = turn_weights(projection_weight)
    joint = pick(pairs, chain_first_residue, gap_embedding, blocks, (weights,))
    cells = lax.all_to_all(joint, "res", split_axis=0, concat_axis=0, tiled=True)
    bias, vectors = order_bias(
        near,
        other,
        order,
        (layer_norm_gain, layer_norm_bias, output_bias, gate_bias_heads),
        (weights, output_weight),
    )
    cells = cells.reshape(members, local_rows // members, local_columns, channels)
    pieces = attend(cells, weights, output_weight, vectors, bias)
    return place(*spread(pieces), (local_rows, local_columns, channels))


def solution(mesh):
    return jax.shard_map(
        local,
        mesh=mesh,
        in_specs=(
            P("rows", "res", None),
            P(None, "rows"),
            P(),
            P(),
            P(),
            P(),
            P(),
            P(),
            P(None, "res", None),
            P(),
            P(),
        ),
        out_specs=P("rows", "res", None),
        check_vma=False,
    )
```

```python
import functools

import jax
import jax.numpy as jnp
from jax import lax
from jax.experimental import pallas as pl
from jax.experimental.pallas import tpu as pltpu
from jax.sharding import PartitionSpec as P

norm_eps = 1e-05
cores = 2


def pick_kernel(owners, pairs_ref, first_ref, gap_ref, *refs):
    blocks, (out_ref, held, sems) = refs[:owners], refs[-3:]
    local_rows, local_columns, channels = blocks[0].shape
    part_rows = out_ref.shape[0]
    pieces = sems.shape[0]
    piece_rows = part_rows // pieces
    chains = first_ref.shape[0]
    shift = local_rows.bit_length() - 1
    assert local_rows == 1 << shift
    me = lax.axis_index("rows")
    start = lax.axis_index("res") * local_columns
    low, high = jnp.int32(0), jnp.int32(0)
    for k in range(1, chains):
        low += (first_ref[k] <= start).astype(jnp.int32)
        high += (first_ref[k] <= start + local_columns - 1).astype(jnp.int32)
    edge = first_ref[high] - start
    in_high = lax.broadcasted_iota(jnp.int32, (local_columns, channels), 0) >= edge
    gap = gap_ref[...].astype(jnp.float32).reshape(1, channels)
    gap = jnp.broadcast_to(gap, (local_columns, channels))
    names = [lax.rem(me - k + owners, owners) for k in range(owners)]

    def cells(row):
        owner = row >> shift
        within = row & (local_rows - 1)
        found = blocks[0][within].astype(jnp.float32)
        for k in range(1, owners):
            found = jnp.where(owner == names[k], blocks[k][within].astype(jnp.float32), found)
        return jnp.where(row >= 0, found, gap)

    copies = []
    for k in range(pieces):
        rows = pl.ds(k * piece_rows, piece_rows)
        for row in range(k * piece_rows, (k + 1) * piece_rows):
            both = jnp.where(in_high, cells(pairs_ref[high, row]), cells(pairs_ref[low, row]))
            held[row] = both.astype(jnp.bfloat16)
        copies.append(pltpu.make_async_copy(held.at[rows], out_ref.at[rows], sems.at[k]))
        copies[-1].start()
    for copy in copies:
        copy.wait()


def pick(pairs, chain_first_residue, gap, blocks, earlier):
    owners = len(blocks)
    local_rows, local_columns, channels = blocks[0].shape
    pieces = 2
    smem = pl.BlockSpec(memory_space=pltpu.SMEM)
    vmem = pl.BlockSpec(memory_space=pltpu.VMEM)
    anywhere = pl.BlockSpec(memory_space=pl.ANY)
    block_bytes = local_rows * local_columns * channels * 2
    shape = blocks[0].shape
    return pl.pallas_call(
        functools.partial(pick_kernel, owners),
        out_shape=jax.ShapeDtypeStruct(shape, jnp.bfloat16),
        in_specs=[smem, smem, vmem] + [vmem] * owners + [anywhere] * len(earlier),
        out_specs=anywhere,
        scratch_shapes=[pltpu.VMEM(shape, jnp.bfloat16), pltpu.SemaphoreType.DMA((pieces,))],
        compiler_params=pltpu.CompilerParams(vmem_limit_bytes=(owners + 4) * block_bytes),
        name="pick_joint",
    )(pairs, chain_first_residue, gap, *blocks, *earlier)


def bias_kernel(order, near_ref, far_ref, *refs):
    rows, gate_ref, (out_ref, vectors_ref, held) = refs[:3], refs[3], refs[-3:]
    me = lax.axis_index("res")
    half, heads, block, _ = near_ref.shape
    for place, flip in enumerate(order):
        source = near_ref if place < half else far_ref
        first = pl.multiple_of((me ^ flip) * block, block)
        held[:, pl.ds(first, block), :] = source[place % half].astype(jnp.float32)

    def one_head(h, carry):
        out_ref[h] = held[h].T
        return carry

    lax.fori_loop(0, heads, one_head, 0)
    width = gate_ref.shape[0]
    for place, ref in enumerate(rows):
        vectors_ref[place : place + 1] = ref[...].astype(jnp.float32).reshape(1, width)
    gate = gate_ref[...].astype(jnp.float32).reshape(1, width)
    vectors_ref[8:] = jnp.broadcast_to(gate, (width, width)).T


def gather_bias(shard):
    members = lax.axis_size("res")

    def swap(piece, flip):
        return lax.ppermute(piece, "res", [(i, i ^ flip) for i in range(members)])

    far, next_far = members // 2, members // 4
    shard = shard[None]
    pieces = [shard]
    order = [0]
    for flip in (far, next_far, far + next_far):
        pieces.append(swap(shard, flip))
        order.append(flip)
    flip = members // 8
    while flip > 1:
        pieces += [swap(piece, flip) for piece in pieces]
        order += [place ^ flip for place in order]
        flip //= 2
    near = jnp.concatenate(pieces, axis=0)
    return near, swap(near, 1), order + [place ^ 1 for place in order]


def order_bias(near, other, order, vectors, earlier):
    half, heads, block, keys = near.shape
    width = vectors[-1].shape[0]
    vmem = pl.BlockSpec(memory_space=pltpu.VMEM)
    anywhere = pl.BlockSpec(memory_space=pl.ANY)
    return pl.pallas_call(
        functools.partial(bias_kernel, order),
        out_shape=[
            jax.ShapeDtypeStruct((heads, keys, 2 * half * block), jnp.float32),
            jax.ShapeDtypeStruct((8 + width, width), jnp.float32),
        ],
        in_specs=[vmem] * (2 + len(vectors)) + [anywhere] * len(earlier),
        out_specs=[vmem] * 2,
        scratch_shapes=[pltpu.VMEM((heads, 2 * half * block, keys), jnp.float32)],
        compiler_params=pltpu.CompilerParams(vmem_limit_bytes=14 << 20),
        name="order_bias",
    )(near, other, *vectors, *earlier)


def weights_kernel(heads, weight_ref, weights_ref):
    width = weight_ref.shape[1] // 4
    depth = width // heads
    turned = weight_ref[...].T
    kinds = []
    for kind in range(4):
        rows = [turned[(h * 4 + kind) * depth : (h * 4 + kind + 1) * depth] for h in range(heads)]
        kinds.append(jnp.concatenate(rows, axis=0))
    for place, kind in enumerate((kinds[0], kinds[2], kinds[3], kinds[1].T)):
        weights_ref[place * width : (place + 1) * width] = kind


def turn_weights(projection_weight):
    channels, heads, four = projection_weight.shape
    width = heads * four // 4
    vmem = pl.BlockSpec(memory_space=pltpu.VMEM)
    return pl.pallas_call(
        functools.partial(weights_kernel, heads),
        out_shape=jax.ShapeDtypeStruct((4 * width, channels), jnp.bfloat16),
        in_specs=[vmem],
        out_specs=vmem,
        compiler_params=pltpu.CompilerParams(vmem_limit_bytes=8 << 20),
        name="turn_weights",
    )(projection_weight.reshape(channels, heads * four))


def attend_kernel(cells_ref, weights_ref, out_weight_ref, vectors_ref, bias_ref, *refs):
    near_refs, far_refs, (staged_ref, scores_ref) = refs[:2], refs[2:-2], refs[-2:]
    senders, rows, block, channels = cells_ref.shape
    me = lax.axis_index("res")
    residues = senders * block
    heads = bias_ref.shape[0]
    width = weights_ref.shape[0] // 4
    depth = width // heads
    ones = jnp.ones((16, residues), jnp.bfloat16)
    group = min(128, width)
    head_of = lax.broadcasted_iota(jnp.int32, (1, group), 1) // depth
    masks = [(head_of == h).astype(jnp.bfloat16) for h in range(group // depth)]

    def begin(r):
        wide = cells_ref[:, r].reshape(residues, channels).astype(jnp.float32)
        center = jnp.mean(wide, axis=-1, keepdims=True)
        wide = wide - center
        spread = jnp.mean(jnp.square(wide), axis=-1, keepdims=True)
        normed = wide * lax.rsqrt(spread + norm_eps) * vectors_ref[0:1] + vectors_ref[1:2]
        normed = normed.astype(jnp.bfloat16)
        keys = jnp.dot(
            normed, weights_ref[3 * width :], preferred_element_type=jnp.float32
        )
        rest = lax.dot_general(
            weights_ref[: 3 * width], normed, (((1,), (1,)), ((), ())),
            preferred_element_type=jnp.float32,
        )
        queries = (rest[:width] * depth**-0.5).astype(jnp.bfloat16)
        values = rest[width : 2 * width].astype(jnp.bfloat16)
        keys = keys.astype(jnp.bfloat16)
        for k in range(width // group):
            lanes = slice(k * group, (k + 1) * group)
            stack = jnp.concatenate([keys[:, lanes] * mask for mask in masks], axis=0)
            scores_ref[r % 2, k] = jnp.dot(
                stack, queries[lanes], preferred_element_type=jnp.float32
            )
        gates = 0.5 + 0.5 * jnp.tanh(0.5 * (rest[2 * width :] + vectors_ref[8:]))
        return values, gates

    def weigh(r, h):
        values, gates = begun[r]
        low, high = h * depth, (h + 1) * depth
        first = low % group // depth * residues
        scores = scores_ref[r % 2, low // group, first : first + residues] + bias_ref[h]
        highest = jnp.max(scores, axis=0, keepdims=True)
        lifted = jnp.exp(scores - highest).astype(jnp.bfloat16)
        left = jnp.concatenate([values[low:high], ones], axis=0)
        summed = jnp.dot(left, lifted, preferred_element_type=jnp.float32)
        inverse = 1.0 / summed[depth : depth + 1]
        return (summed[:depth] * (gates[low:high] * inverse)).astype(jnp.bfloat16)

    def finish(r, heads_out):
        attended = jnp.concatenate(heads_out, axis=0).T
        update = jnp.dot(attended, out_weight_ref[...], preferred_element_type=jnp.float32)
        update = (update + vectors_ref[2:3]).astype(jnp.bfloat16)
        staged_ref[...] = update.reshape(senders, block, channels)
        for flip in range(senders):
            chip, core = flip // cores, flip % cores
            if chip < 4:
                near_refs[chip // 2][chip % 2, core, r] = staged_ref[me ^ flip]
            else:
                far_refs[chip - 4][core, r] = staged_ref[me ^ flip]

    begun = {0: begin(0)}
    done = {r: [] for r in range(rows)}
    for r in range(rows):
        for h in range(heads):
            if h == heads // 2 and r + 1 < rows:
                begun[r + 1] = begin(r + 1)
            done[r].append(weigh(r, h))
            if h == 0 and r:
                finish(r - 1, done[r - 1])
    finish(rows - 1, done[rows - 1])


def attend(cells, weights, out_weight, vectors, bias):
    heads, residues, _ = bias.shape
    senders, rows, block, channels = cells.shape
    width = weights.shape[0] // 4
    group = min(128, width)
    vmem = pl.BlockSpec(memory_space=pltpu.VMEM)
    score_shape = (2, width // group, heads * group // width * residues, residues)
    one = (cores, rows, block, channels)
    shapes = [(2, *one)] * 2 + [one] * (senders // cores - 4)
    return pl.pallas_call(
        attend_kernel,
        out_shape=[jax.ShapeDtypeStruct(shape, jnp.bfloat16) for shape in shapes],
        in_specs=[vmem] * 5,
        out_specs=[vmem] * len(shapes),
        scratch_shapes=[
            pltpu.VMEM((senders, block, channels), jnp.bfloat16),
            pltpu.VMEM(score_shape, jnp.float32),
        ],
        compiler_params=pltpu.CompilerParams(vmem_limit_bytes=24 << 20),
        name="attend_rows",
    )(cells, weights, out_weight, vectors, bias)


def swap(array, flip):
    members = lax.axis_size("res")
    return lax.ppermute(array, "res", [(i, i ^ flip) for i in range(members)])


def spread(pieces):
    here, there, far = pieces[0], pieces[1], pieces[2:]
    far = [swap(piece, (4 + k) * cores) for k, piece in enumerate(far)]
    there = swap(there, 2 * cores)
    hop = swap(jnp.stack([here[1], there[1]]), cores)
    arrived = [(2, there[0]), *((4 + k, piece) for k, piece in enumerate(far))]
    arrived += [(1, hop[0]), (3, hop[1]), (0, here[0])]
    other = swap(jnp.stack([blocks[1] for _, blocks in arrived]), 1)
    return [chip for chip, _ in arrived], far, there, hop, here, other


def place_kernel(order, *refs):
    far_refs, (there_ref, hop_ref, here_ref, other_ref, out_ref, sems) = refs[:-6], refs[-6:]
    me = lax.axis_index("res")
    rows = other_ref.shape[1]
    near = [here_ref.at[0, 0], hop_ref.at[0, 0], there_ref.at[0, 0], hop_ref.at[1, 0]]
    copies = []
    for k, chip in enumerate(order):
        same = near[chip] if chip < 4 else far_refs[chip - 4].at[0]
        for core, source in enumerate((same, other_ref.at[k])):
            first = (me ^ (chip * cores + core)) * rows
            target = out_ref.at[pl.ds(first, rows)]
            copies.append(pltpu.make_async_copy(source, target, sems.at[len(copies)]))
    for copy in copies:
        copy.start()
    for copy in copies:
        copy.wait()


def place(order, far, there, hop, here, other, shape):
    vmem = pl.BlockSpec(memory_space=pltpu.VMEM)
    return pl.pallas_call(
        functools.partial(place_kernel, order),
        out_shape=jax.ShapeDtypeStruct(shape, jnp.bfloat16),
        in_specs=[vmem] * (len(far) + 4),
        out_specs=pl.BlockSpec(memory_space=pl.ANY),
        scratch_shapes=[pltpu.SemaphoreType.DMA((cores * len(order),))],
        compiler_params=pltpu.CompilerParams(vmem_limit_bytes=8 << 20),
        name="place_rows",
    )(*far, there, hop, here, other)


def local(
    source_alignment_rows,
    pairs,
    chain_first_residue,
    gap_embedding,
    layer_norm_gain,
    layer_norm_bias,
    projection_weight,
    gate_bias_heads,
    pair_bias_logits,
    output_weight,
    output_bias,
):
    local_rows, local_columns, channels = source_alignment_rows.shape
    owners = lax.axis_size("rows")
    members = lax.axis_size("res")
    near, other, order = gather_bias(pair_bias_logits)
    blocks = [source_alignment_rows]
    for hop in range(1, owners):
        blocks.append(
            lax.ppermute(
                source_alignment_rows, "rows", [(i, (i + hop) % owners) for i in range(owners)]
            )
        )
    weights = turn_weights(projection_weight)
    joint = pick(pairs, chain_first_residue, gap_embedding, blocks, (weights,))
    cells = lax.all_to_all(joint, "res", split_axis=0, concat_axis=0, tiled=True)
    bias, vectors = order_bias(
        near,
        other,
        order,
        (layer_norm_gain, layer_norm_bias, output_bias, gate_bias_heads),
        (weights, output_weight),
    )
    cells = cells.reshape(members, local_rows // members, local_columns, channels)
    pieces = attend(cells, weights, output_weight, vectors, bias)
    return place(*spread(pieces), (local_rows, local_columns, channels))


def solution(mesh):
    return jax.shard_map(
        local,
        mesh=mesh,
        in_specs=(
            P("rows", "res", None),
            P(None, "rows"),
            P(),
            P(),
            P(),
            P(),
            P(),
            P(),
            P(None, "res", None),
            P(),
            P(),
        ),
        out_specs=P("rows", "res", None),
        check_vma=False,
    )
```

```python
import functools

import jax
import jax.numpy as jnp
from jax import lax
from jax.experimental import pallas as pl
from jax.experimental.pallas import tpu as pltpu
from jax.sharding import PartitionSpec as P

norm_eps = 1e-05
cores = 2


def piece_of(refs, flip):
    chip, core = flip // cores, flip % cores
    if chip < 4:
        return refs[chip // 2].at[chip % 2, core]
    return refs[chip - 2].at[core]


def piece_shapes(members, rows, block, channels):
    one = (cores, rows, block, channels)
    shapes = [(2, *one)] * 2 + [one] * (members // cores - 4)
    return [jax.ShapeDtypeStruct(shape, jnp.bfloat16) for shape in shapes]


def pick_kernel(owners, members, pairs_ref, first_ref, gap_ref, *refs):
    blocks, out_refs = refs[:owners], refs[-(members // cores - 2) :]
    local_rows, local_columns, channels = blocks[0].shape
    rows = local_rows // members
    chains = first_ref.shape[0]
    shift = local_rows.bit_length() - 1
    assert local_rows == 1 << shift
    me = lax.axis_index("rows")
    place = lax.axis_index("res")
    start = place * local_columns
    low, high = jnp.int32(0), jnp.int32(0)
    for k in range(1, chains):
        low += (first_ref[k] <= start).astype(jnp.int32)
        high += (first_ref[k] <= start + local_columns - 1).astype(jnp.int32)
    edge = first_ref[high] - start
    in_high = lax.broadcasted_iota(jnp.int32, (local_columns, channels), 0) >= edge
    gap = gap_ref[...].astype(jnp.float32).reshape(1, channels)
    gap = jnp.broadcast_to(gap, (local_columns, channels))
    names = [lax.rem(me - k + owners, owners) for k in range(owners)]

    def cells(row):
        owner = row >> shift
        within = row & (local_rows - 1)
        found = blocks[0][within].astype(jnp.float32)
        for k in range(1, owners):
            found = jnp.where(owner == names[k], blocks[k][within].astype(jnp.float32), found)
        return jnp.where(row >= 0, found, gap)

    for flip in range(members):
        first_row = (place ^ flip) * rows
        for i in range(rows):
            row = first_row + i
            both = jnp.where(in_high, cells(pairs_ref[high, row]), cells(pairs_ref[low, row]))
            piece_of(out_refs, flip)[i] = both.astype(jnp.bfloat16)


def pick(members, pairs, chain_first_residue, gap, blocks, earlier):
    owners = len(blocks)
    local_rows, local_columns, channels = blocks[0].shape
    smem = pl.BlockSpec(memory_space=pltpu.SMEM)
    vmem = pl.BlockSpec(memory_space=pltpu.VMEM)
    anywhere = pl.BlockSpec(memory_space=pl.ANY)
    block_bytes = local_rows * local_columns * channels * 2
    shapes = piece_shapes(members, local_rows // members, local_columns, channels)
    return pl.pallas_call(
        functools.partial(pick_kernel, owners, members),
        out_shape=shapes,
        in_specs=[smem, smem, vmem] + [vmem] * owners + [anywhere] * len(earlier),
        out_specs=[vmem] * len(shapes),
        compiler_params=pltpu.CompilerParams(vmem_limit_bytes=(owners + 4) * block_bytes),
        name="pick_joint",
    )(pairs, chain_first_residue, gap, *blocks, *earlier)


def bias_kernel(order, near_ref, far_ref, *refs):
    rows, gate_ref, (out_ref, vectors_ref, held) = refs[:3], refs[3], refs[-3:]
    me = lax.axis_index("res")
    half, heads, block, keys = near_ref.shape
    for place, flip in enumerate(order):
        source = near_ref if place < half else far_ref
        held[:, flip * block : (flip + 1) * block, :] = source[place % half].astype(jnp.float32)

    def one_head(h, carry):
        turned = held[h].T
        for owner in range(keys // block):
            first = pl.multiple_of((me ^ owner) * block, block)
            out_ref[h, pl.ds(first, block), :] = turned[owner * block : (owner + 1) * block]
        return carry

    lax.fori_loop(0, heads, one_head, 0)
    width = gate_ref.shape[0]
    for place, ref in enumerate(rows):
        vectors_ref[place : place + 1] = ref[...].astype(jnp.float32).reshape(1, width)
    gate = gate_ref[...].astype(jnp.float32).reshape(1, width)
    vectors_ref[8:] = jnp.broadcast_to(gate, (width, width)).T


def gather_lines(shard):
    far, next_far = lax.axis_size("res") // 2, lax.axis_size("res") // 4
    shard = shard[None]
    order = [0, far, next_far, far + next_far]
    return jnp.concatenate([shard, *(swap(shard, flip) for flip in order[1:])], axis=0), order


def gather_bias(held, order):
    flip = lax.axis_size("res") // 8
    while flip >= cores:
        held = jnp.concatenate([held, swap(held, flip)], axis=0)
        order = order + [flip ^ place for place in order]
        flip //= 2
    return held, swap(held, 1), order + [1 ^ place for place in order]


def same_kernel(*refs):
    pass


def after(array, *earlier):
    anywhere = pl.BlockSpec(memory_space=pl.ANY)
    return pl.pallas_call(
        same_kernel,
        out_shape=jax.ShapeDtypeStruct(array.shape, array.dtype),
        in_specs=[anywhere] * (1 + len(earlier)),
        out_specs=anywhere,
        input_output_aliases={0: 0},
        name="same_cells",
    )(array, *earlier)


def order_bias(near, other, order, vectors, earlier):
    half, heads, block, keys = near.shape
    width = vectors[-1].shape[0]
    vmem = pl.BlockSpec(memory_space=pltpu.VMEM)
    anywhere = pl.BlockSpec(memory_space=pl.ANY)
    return pl.pallas_call(
        functools.partial(bias_kernel, order),
        out_shape=[
            jax.ShapeDtypeStruct((heads, keys, 2 * half * block), jnp.float32),
            jax.ShapeDtypeStruct((8 + width, width), jnp.float32),
        ],
        in_specs=[vmem] * (2 + len(vectors)) + [anywhere] * len(earlier),
        out_specs=[vmem] * 2,
        scratch_shapes=[pltpu.VMEM((heads, 2 * half * block, keys), jnp.float32)],
        compiler_params=pltpu.CompilerParams(vmem_limit_bytes=14 << 20),
        name="order_bias",
    )(near, other, *vectors, *earlier)


def weights_kernel(heads, weight_ref, weights_ref):
    width = weight_ref.shape[1] // 4
    depth = width // heads
    turned = weight_ref[...].T
    kinds = []
    for kind in range(4):
        rows = [turned[(h * 4 + kind) * depth : (h * 4 + kind + 1) * depth] for h in range(heads)]
        kinds.append(jnp.concatenate(rows, axis=0))
    for place, kind in enumerate((kinds[0], kinds[2], kinds[3], kinds[1].T)):
        weights_ref[place * width : (place + 1) * width] = kind


def turn_weights(projection_weight):
    channels, heads, four = projection_weight.shape
    width = heads * four // 4
    vmem = pl.BlockSpec(memory_space=pltpu.VMEM)
    return pl.pallas_call(
        functools.partial(weights_kernel, heads),
        out_shape=jax.ShapeDtypeStruct((4 * width, channels), jnp.bfloat16),
        in_specs=[vmem],
        out_specs=vmem,
        compiler_params=pltpu.CompilerParams(vmem_limit_bytes=8 << 20),
        name="turn_weights",
    )(projection_weight.reshape(channels, heads * four))


def arrived_from(order, refs, flip):
    far_refs, (there_ref, hop_ref, here_ref, other_ref) = refs[:-4], refs[-4:]
    chip, core = flip // cores, flip % cores
    if core:
        return other_ref.at[order.index(chip)]
    if chip >= 4:
        return far_refs[chip - 4].at[0]
    near = (here_ref.at[0, 0], hop_ref.at[0, 0], there_ref.at[0, 0], hop_ref.at[1, 0])
    return near[chip]


def attend_kernel(order, weights_ref, out_weight_ref, vectors_ref, bias_ref, *refs):
    arrived, out_refs, scores_ref = refs[: len(order)], refs[len(order) : -1], refs[-1]
    senders = len(order) * cores
    rows, block, channels = arrived_from(order, arrived, 0).shape
    residues = senders * block
    heads = bias_ref.shape[0]
    width = weights_ref.shape[0] // 4
    depth = width // heads
    ones = jnp.ones((16, residues), jnp.bfloat16)
    group = min(128, width)
    head_of = lax.broadcasted_iota(jnp.int32, (1, group), 1) // depth
    masks = [(head_of == h).astype(jnp.bfloat16) for h in range(group // depth)]

    def begin(r):
        wide = [arrived_from(order, arrived, flip)[r] for flip in range(senders)]
        wide = jnp.concatenate(wide, axis=0).astype(jnp.float32)
        center = jnp.mean(wide, axis=-1, keepdims=True)
        wide = wide - center
        spread = jnp.mean(jnp.square(wide), axis=-1, keepdims=True)
        normed = wide * lax.rsqrt(spread + norm_eps) * vectors_ref[0:1] + vectors_ref[1:2]
        normed = normed.astype(jnp.bfloat16)
        keys = jnp.dot(
            normed, weights_ref[3 * width :], preferred_element_type=jnp.float32
        )
        rest = lax.dot_general(
            weights_ref[: 3 * width], normed, (((1,), (1,)), ((), ())),
            preferred_element_type=jnp.float32,
        )
        queries = (rest[:width] * depth**-0.5).astype(jnp.bfloat16)
        values = rest[width : 2 * width].astype(jnp.bfloat16)
        keys = keys.astype(jnp.bfloat16)
        for k in range(width // group):
            lanes = slice(k * group, (k + 1) * group)
            stack = jnp.concatenate([keys[:, lanes] * mask for mask in masks], axis=0)
            scores_ref[r % 2, k] = jnp.dot(
                stack, queries[lanes], preferred_element_type=jnp.float32
            )
        gates = 0.5 + 0.5 * jnp.tanh(0.5 * (rest[2 * width :] + vectors_ref[8:]))
        return values, gates

    def weigh(r, h):
        values, gates = begun[r]
        low, high = h * depth, (h + 1) * depth
        first = low % group // depth * residues
        scores = scores_ref[r % 2, low // group, first : first + residues] + bias_ref[h]
        highest = jnp.max(scores, axis=0, keepdims=True)
        lifted = jnp.exp(scores - highest).astype(jnp.bfloat16)
        left = jnp.concatenate([values[low:high], ones], axis=0)
        summed = jnp.dot(left, lifted, preferred_element_type=jnp.float32)
        inverse = 1.0 / summed[depth : depth + 1]
        return (summed[:depth] * (gates[low:high] * inverse)).astype(jnp.bfloat16)

    def finish(r, heads_out):
        attended = jnp.concatenate(heads_out, axis=0).T
        update = jnp.dot(attended, out_weight_ref[...], preferred_element_type=jnp.float32)
        update = (update + vectors_ref[2:3]).astype(jnp.bfloat16)
        for flip in range(senders):
            piece_of(out_refs, flip)[r] = update[flip * block : (flip + 1) * block]

    begun = {0: begin(0)}
    done = {r: [] for r in range(rows)}
    for r in range(rows):
        for h in range(heads):
            if h == heads // 2 and r + 1 < rows:
                begun[r + 1] = begin(r + 1)
            done[r].append(weigh(r, h))
            if h == 0 and r:
                finish(r - 1, done[r - 1])
    finish(rows - 1, done[rows - 1])


def attend(order, arrived, weights, out_weight, vectors, bias):
    heads, residues, _ = bias.shape
    rows, block, channels = arrived[-1].shape[1:]
    width = weights.shape[0] // 4
    group = min(128, width)
    vmem = pl.BlockSpec(memory_space=pltpu.VMEM)
    score_shape = (2, width // group, heads * group // width * residues, residues)
    shapes = piece_shapes(residues // block, rows, block, channels)
    return pl.pallas_call(
        functools.partial(attend_kernel, order),
        out_shape=shapes,
        in_specs=[vmem] * (4 + len(arrived)),
        out_specs=[vmem] * len(shapes),
        scratch_shapes=[pltpu.VMEM(score_shape, jnp.float32)],
        compiler_params=pltpu.CompilerParams(vmem_limit_bytes=24 << 20),
        name="attend_rows",
    )(weights, out_weight, vectors, bias, *arrived)


def swap(array, flip):
    members = lax.axis_size("res")
    return lax.ppermute(array, "res", [(i, i ^ flip) for i in range(members)])


def spread(pieces):
    here, there, far = pieces[0], pieces[1], pieces[2:]
    far = [swap(piece, (4 + k) * cores) for k, piece in enumerate(far)]
    there = swap(there, 2 * cores)
    hop = swap(jnp.stack([here[1], there[1]]), cores)
    arrived = [(2, there[0]), *((4 + k, piece) for k, piece in enumerate(far))]
    arrived += [(1, hop[0]), (3, hop[1]), (0, here[0])]
    other = swap(jnp.stack([blocks[1] for _, blocks in arrived]), 1)
    return [chip for chip, _ in arrived], [*far, there, hop, here, other]


def place_kernel(order, *refs):
    arrived, (out_ref, sems) = refs[:-2], refs[-2:]
    me = lax.axis_index("res")
    rows = arrived[-1].shape[1]
    copies = [
        pltpu.make_async_copy(
            arrived_from(order, arrived, flip),
            out_ref.at[pl.ds((me ^ flip) * rows, rows)],
            sems.at[flip],
        )
        for flip in range(len(order) * cores)
    ]
    for copy in copies:
        copy.start()
    for copy in copies:
        copy.wait()


def place(order, arrived, shape):
    vmem = pl.BlockSpec(memory_space=pltpu.VMEM)
    return pl.pallas_call(
        functools.partial(place_kernel, order),
        out_shape=jax.ShapeDtypeStruct(shape, jnp.bfloat16),
        in_specs=[vmem] * len(arrived),
        out_specs=pl.BlockSpec(memory_space=pl.ANY),
        scratch_shapes=[pltpu.SemaphoreType.DMA((cores * len(order),))],
        compiler_params=pltpu.CompilerParams(vmem_limit_bytes=8 << 20),
        name="place_rows",
    )(*arrived)


def local(
    source_alignment_rows,
    pairs,
    chain_first_residue,
    gap_embedding,
    layer_norm_gain,
    layer_norm_bias,
    projection_weight,
    gate_bias_heads,
    pair_bias_logits,
    output_weight,
    output_bias,
):
    local_rows, local_columns, channels = source_alignment_rows.shape
    owners = lax.axis_size("rows")
    members = lax.axis_size("res")
    held, lines = gather_lines(pair_bias_logits)
    blocks = [source_alignment_rows]
    for hop in range(1, owners):
        blocks.append(
            lax.ppermute(
                source_alignment_rows, "rows", [(i, (i + hop) % owners) for i in range(owners)]
            )
        )
    weights = turn_weights(projection_weight)
    picked = pick(members, pairs, chain_first_residue, gap_embedding, blocks, (weights,))
    chips, cells = spread(picked)
    near, other, order = gather_bias(after(held, picked[0]), lines)
    bias, vectors = order_bias(
        near,
        other,
        order,
        (layer_norm_gain, layer_norm_bias, output_bias, gate_bias_heads),
        (weights, output_weight),
    )
    pieces = attend(chips, cells, weights, output_weight, vectors, bias)
    return place(*spread(pieces), (local_rows, local_columns, channels))


def solution(mesh):
    return jax.shard_map(
        local,
        mesh=mesh,
        in_specs=(
            P("rows", "res", None),
            P(None, "rows"),
            P(),
            P(),
            P(),
            P(),
            P(),
            P(),
            P(None, "res", None),
            P(),
            P(),
        ),
        out_specs=P("rows", "res", None),
        check_vma=False,
    )
```
